32 devices in a mesh: group: 16 (over z, x, core), head: 2 (over y).
Axes of the slice: x: 2, y: 2, z: 4, core: 2. Of those that a mesh axis runs over, the one named last changes fastest.
Arguments:
- tokens: bfloat16 [1024, 3072], P(('group', 'head')), may hold values from -10 to 10
- attn_gain: float32 [3072], replicated, may hold values from 0.25 to 1.75
- w_query: bfloat16 [3072, 1536], P('group', 'head'), may hold values from -1 to 1
- w_key: bfloat16 [3072, 1536], P('group', 'head'), may hold values from -1 to 1
- w_value: bfloat16 [3072, 1536], P('group', 'head'), may hold values from -0.109375 to 0.109375
- w_out: bfloat16 [1536, 3072], P('head', 'group'), may hold values from -0.15625 to 0.15625
- mlp_gain: float32 [3072], replicated, may hold values from 0.25 to 1.75
- w_gate: bfloat16 [3072, 4096], P('group', 'head'), may hold values from -0.109375 to 0.109375
- w_up: bfloat16 [3072, 4096], P('group', 'head'), may hold values from -0.109375 to 0.109375
- w_down: bfloat16 [4096, 3072], P('head', 'group'), may hold values from -0.09375 to 0.09375
- segment_ids: int32 [16, 64], P('group'), may hold values from 0 to 3, never falling along the last dimension, each value on 1 to 32 neighbouring positions
- cache_slot: int32 [16, 64], P('group'), may hold values from 0 to 63, each once within a row
Outputs:
- layer_out: bfloat16 [1024, 3072], P(('group', 'head'))
- cache_keys: bfloat16 [1024, 1536], P('group', 'head')
- cache_values: bfloat16 [1024, 1536], P('group', 'head')
The draws below stay inside these ranges and needn't reach their ends.
Inputs may be any that keep to these rules, and one draw needn't show every extreme that they name: `segment_ids`: within each group, segment ids never fall; each of the 4 prompts has 1 to 32 tokens and one has exactly 32. `cache_slot`: each group's row of cache slots holds every slot once.
All inputs are finite; a program needn't handle non-finite values.
Results may differ from the reference program's by a relative error of at most 0.018.
Values may be sent and summed in bfloat16 or wider, within the bound.
No kernel may reach another device: no remote copies, remote signals or barrier semaphores. Data moves between devices by JAX's collectives and lax.ppermute only.
A program may use at most 128 MiB of HBM per device.

```python
import math
import jax
import jax.numpy as jnp
import numpy as np
from jax import lax

D = 3072
HEAD_DIM = 96
HEADS = 16
FFW = 4096
SEGS = 4
GROUPS = 16
GRP_TOK = 64
TOKENS = 1024
SEG_MOST = 32
N_HEAD = 2


def drawn_weight(key, salt):
    noise = jax.random.truncated_normal(jax.random.fold_in(key, salt), -6.0, 6.0, (D, HEADS * HEAD_DIM), jnp.float32)
    weight = noise * float(D) ** (-0.5)
    return weight


def draw_w_query(key, part):
    return drawn_weight(key, 101).astype(jnp.bfloat16)


def draw_w_key(key, part):
    return drawn_weight(key, 102).astype(jnp.bfloat16)


def draw_tokens(key, part):
    noise = jax.random.truncated_normal(jax.random.fold_in(key, 103), -6.0, 6.0, (TOKENS, D), jnp.float32)
    return noise.astype(jnp.bfloat16)


def levels(stream_key, shape, pieces, smallest, largest):
    def one(dim, parts):
        heights = jax.random.uniform(jax.random.fold_in(jax.random.fold_in(stream_key, 6), dim), (parts,), jnp.float32, smallest / len(pieces), largest / len(pieces))
        return jnp.repeat(jnp.exp(heights), shape[dim] // parts).reshape((-1,) + (1,) * (len(shape) - dim - 1))

    factor_of = one(*pieces[0])
    for cut in pieces[1:]:
        factor_of = factor_of * one(*cut)
    return factor_of


def length_profile(count, total, most, skew):
    loads = [(1 << 20) // math.isqrt(rank ** skew) + 1 for rank in range(2, count + 1)]
    spare, holding = total - most - (count - 1), [1] * (count - 1)
    while spare > 0:
        movable = [i for i in range(count - 1) if holding[i] < most]
        whole, remaining = sum([loads[i] for i in movable]), spare
        for i in movable:
            extra = min(most - holding[i], max(1, remaining * loads[i] // whole), spare)
            holding[i] = holding[i] + extra
            spare = spare - extra
    return np.array([most] + holding)


def ragged(stream_key, amount, total, most, lean):
    if amount == 2:
        one = jax.random.randint(stream_key, (), max(1, total - most), min(most, total - 1) + 1)
        return jnp.stack([one, total - one])
    tallies = jnp.asarray(length_profile(amount, total, most, lean), jnp.int32)
    twos = (amount - 1) // 2
    giver, sink = tallies[1:1 + 2 * twos:2], tallies[2:2 + 2 * twos:2]
    room = jnp.minimum(giver - 1, most - sink)
    shifted = jax.random.randint(jax.random.fold_in(stream_key, 1), (twos,), 0, 1 << 20) % (room + 1)
    tallies = tallies.at[1:1 + 2 * twos:2].set(giver - shifted).at[2:2 + 2 * twos:2].set(sink + shifted)
    return tallies[jax.random.permutation(jax.random.fold_in(stream_key, 2), amount)]


def normal_values(key, dims, deviation, reach, shards=(), kind=jnp.bfloat16):
    entries = jax.random.normal(key, dims, jnp.float32) * deviation
    if len(shards) > 0:
        entries = levels(key, dims, shards, -0.22, 0.18) * entries
    return jnp.clip(entries, min=-reach, max=reach).astype(kind)


def setup_inputs(seed: int = 0) -> dict:
    arg_keys = jax.random.split(jax.random.key(seed), 13)
    return {
        "tokens": draw_tokens(jax.random.fold_in(arg_keys[12], 71), 0),
        "attn_gain": jnp.clip(1.0 + 0.15 * jax.random.normal(arg_keys[1], (D,), jnp.float32), 0.25, 1.75),
        "w_query": draw_w_query(jax.random.fold_in(arg_keys[12], 71), 0),
        "w_key": draw_w_key(jax.random.fold_in(arg_keys[12], 71), 0),
        "w_value": normal_values(arg_keys[4], (D, HEADS * HEAD_DIM), D ** -0.5, 0.109375, ((0, 16), (1, 2))),
        "w_out": normal_values(arg_keys[5], (HEADS * HEAD_DIM, D), (HEADS * HEAD_DIM) ** -0.5, 0.15625, ((0, 2), (1, 16))),
        "mlp_gain": jnp.clip(1.0 + 0.15 * jax.random.normal(arg_keys[6], (D,), jnp.float32), 0.25, 1.75),
        "w_gate": normal_values(arg_keys[7], (D, FFW), D ** -0.5, 0.109375, ((0, 16), (1, 2))),
        "w_up": normal_values(arg_keys[8], (D, FFW), D ** -0.5, 0.109375, ((0, 16), (1, 2))),
        "w_down": normal_values(arg_keys[9], (FFW, D), FFW ** -0.5, 0.09375, ((0, 2), (1, 16))),
        "segment_ids": jax.vmap(lambda own: jnp.searchsorted(jnp.cumsum(ragged(own, SEGS, GRP_TOK, SEG_MOST, 2)), jnp.arange(GRP_TOK), side="right"))(jax.random.split(arg_keys[10], GROUPS)).reshape((GROUPS, GRP_TOK)).astype(jnp.int32),
        "cache_slot": jax.vmap(lambda own: jax.random.permutation(own, GRP_TOK))(jax.random.split(arg_keys[11], GROUPS)).reshape((GROUPS, GRP_TOK)).astype(jnp.int32),
    }


def norm_rows(rows, gain):
    values = rows.astype(jnp.float32)
    scale = lax.rsqrt(lax.optimization_barrier(jnp.mean(values * values, axis=-1, keepdims=True)) + 1e-05)
    return (values * scale * gain.astype(jnp.float32)).astype(jnp.bfloat16)

def positions(segment):
    count = segment.shape[0]
    index = jnp.arange(count, dtype=jnp.int32)
    before = jnp.concatenate([jnp.full((1,), -1, jnp.int32), segment[:-1].astype(jnp.int32)])
    starts = jnp.where(segment.astype(jnp.int32) != before, index, jnp.zeros_like(index))
    return index - lax.cummax(starts, axis=0)

def rotate(heads, place):
    half = heads.shape[-1] // 2
    freq = 10000.0 ** (-2.0 * jnp.arange(half, dtype=jnp.float32) / heads.shape[-1])
    angle = place.astype(jnp.float32)[:, None] * freq[None, :]
    cosine = jnp.cos(angle)[:, None, :]
    sine = jnp.sin(angle)[:, None, :]
    first = heads[..., :half]
    second = heads[..., half:]
    return jnp.concatenate([first * cosine - second * sine, second * cosine + first * sine], axis=-1)

def attend_group(inputs):
    query, key, value, segment = inputs
    count = segment.shape[0]
    index = jnp.arange(count, dtype=jnp.int32)
    allowed = (segment[:, None] == segment[None, :]) & (index[None, :] <= index[:, None])
    scores = jnp.einsum('qhd,khd->hqk', query.astype(jnp.float32), key.astype(jnp.float32))
    scores = scores * (1.0 / HEAD_DIM ** 0.5)
    scores = jnp.where(allowed[None, :, :], scores, -1e+30)
    top = lax.optimization_barrier(jnp.max(scores, axis=-1, keepdims=True))
    expo = jnp.exp(scores - top)
    probs = (expo / lax.optimization_barrier(jnp.sum(expo, axis=-1, keepdims=True))).astype(jnp.bfloat16)
    mixed = jnp.einsum('hqk,khd->qhd', probs.astype(jnp.float32), value.astype(jnp.float32))
    return mixed.astype(jnp.bfloat16)

def place_cache(rows, slots):
    return jnp.zeros_like(rows).at[slots].set(rows)

def block_sum(left, right, blocks):
    width = left.shape[1] // blocks
    total = jnp.zeros((left.shape[0], right.shape[1]), jnp.float32)
    for block in range(blocks):
        part = jnp.dot(left[:, block * width:(block + 1) * width], right[block * width:(block + 1) * width, :], preferred_element_type=jnp.float32)
        total = total + lax.optimization_barrier(part.astype(jnp.bfloat16)).astype(jnp.float32)
    return total

def reference(tokens, attn_gain, w_query, w_key, w_value, w_out, mlp_gain, w_gate, w_up, w_down, segment_ids, cache_slot):
    normed = norm_rows(tokens, attn_gain)
    query = jnp.dot(normed, w_query, preferred_element_type=jnp.float32)
    key = jnp.dot(normed, w_key, preferred_element_type=jnp.float32)
    value = jnp.dot(normed, w_value, preferred_element_type=jnp.float32)
    place = jax.vmap(positions)(segment_ids).reshape(-1)
    q_rot = rotate(query.reshape(TOKENS, HEADS, HEAD_DIM), place).astype(jnp.bfloat16)
    k_rot = rotate(key.reshape(TOKENS, HEADS, HEAD_DIM), place).astype(jnp.bfloat16)
    v_b = value.astype(jnp.bfloat16).reshape(TOKENS, HEADS, HEAD_DIM)
    width = HEADS * HEAD_DIM
    cache_keys = jax.vmap(place_cache)(k_rot.reshape(GROUPS, GRP_TOK, width), cache_slot).reshape(TOKENS, width)
    cache_values = jax.vmap(place_cache)(v_b.reshape(GROUPS, GRP_TOK, width), cache_slot).reshape(TOKENS, width)
    shaped = (q_rot.reshape(GROUPS, GRP_TOK, HEADS, HEAD_DIM), k_rot.reshape(GROUPS, GRP_TOK, HEADS, HEAD_DIM), v_b.reshape(GROUPS, GRP_TOK, HEADS, HEAD_DIM), segment_ids)
    attended = lax.map(attend_group, shaped).reshape(TOKENS, width)
    attn_sum = block_sum(attended, w_out, N_HEAD)
    middle = (tokens.astype(jnp.float32) + attn_sum).astype(jnp.bfloat16)
    normed2 = norm_rows(middle, mlp_gain)
    gate = jnp.dot(normed2, w_gate, preferred_element_type=jnp.float32)
    up = jnp.dot(normed2, w_up, preferred_element_type=jnp.float32)
    hidden = (jax.nn.silu(gate) * up).astype(jnp.bfloat16)
    mlp_sum = block_sum(hidden, w_down, N_HEAD)
    layer_out = (middle.astype(jnp.float32) + mlp_sum).astype(jnp.bfloat16)
    return (layer_out, cache_keys, cache_values)
```

```python
import jax
import jax.numpy as jnp
from jax import lax
from jax.sharding import PartitionSpec as P

HEAD_DIM = 96
EPS = 1e-05
OCT = 8
BF = jnp.bfloat16
F32 = jnp.float32


def norm_rows(rows, gain):
    values = rows.astype(F32)
    scale = lax.rsqrt(jnp.mean(values * values, axis=-1, keepdims=True) + EPS)
    return (values * scale * gain).astype(BF)


def positions(segment):
    count = segment.shape[0]
    index = jnp.arange(count, dtype=jnp.int32)
    before = jnp.concatenate([jnp.full((1,), -1, jnp.int32), segment[:-1]])
    starts = jnp.where(segment != before, index, jnp.zeros_like(index))
    return index - lax.cummax(starts, axis=0)


def rotate(heads, place):
    half = heads.shape[-1] // 2
    freq = 10000.0 ** (-2.0 * jnp.arange(half, dtype=F32) / heads.shape[-1])
    angle = place.astype(F32)[:, None] * freq[None, :]
    cosine = jnp.cos(angle)[:, None, :]
    sine = jnp.sin(angle)[:, None, :]
    first = heads[..., :half]
    second = heads[..., half:]
    return jnp.concatenate(
        [first * cosine - second * sine, second * cosine + first * sine], axis=-1
    )


def dot(a, b):
    return jnp.dot(a, b, preferred_element_type=F32)


def attention(query, key, v_b, segment, slots):
    count, width = v_b.shape
    heads_here = width // HEAD_DIM
    index = jnp.arange(count, dtype=jnp.int32)
    place = positions(segment)
    q_rot = rotate(query.reshape(count, heads_here, HEAD_DIM), place).astype(BF)
    k_rot = rotate(key.reshape(count, heads_here, HEAD_DIM), place).astype(BF)
    k_flat = k_rot.reshape(count, width)
    cache_keys = jnp.zeros_like(k_flat).at[slots].set(k_flat)
    cache_values = jnp.zeros_like(v_b).at[slots].set(v_b)
    allowed = (segment[:, None] == segment[None, :]) & (index[None, :] <= index[:, None])
    scores = jnp.einsum("qhd,khd->hqk", q_rot, k_rot, preferred_element_type=F32)
    scores = scores * (1.0 / HEAD_DIM**0.5)
    scores = jnp.where(allowed[None, :, :], scores, -1e30)
    top = jnp.max(scores, axis=-1, keepdims=True)
    expo = jnp.exp(scores - top)
    probs = (expo / jnp.sum(expo, axis=-1, keepdims=True)).astype(BF)
    v_heads = v_b.reshape(count, heads_here, HEAD_DIM)
    attended = jnp.einsum("hqk,khd->qhd", probs, v_heads, preferred_element_type=F32)
    return attended.astype(BF).reshape(count, width), cache_keys, cache_values


def gathered_plan(
    tokens, attn_gain, w_query, w_key, w_value, w_out, mlp_gain, w_gate, w_up, w_down, segment_ids, cache_slot,
):
    whole = lax.all_gather(norm_rows(tokens, attn_gain), "head", axis=0, tiled=True)
    query, key, value = (
        dot(whole, lax.all_gather(w, "group", axis=0, tiled=True)) for w in (w_query, w_key, w_value)
    )
    attended, cache_keys, cache_values = attention(
        query, key, value.astype(BF), segment_ids[0], cache_slot[0]
    )
    out_terms = dot(attended, lax.all_gather(w_out, "group", axis=1, tiled=True))
    attn_rows = lax.psum_scatter(out_terms.astype(BF), "head", scatter_dimension=0, tiled=True)
    middle = (tokens.astype(F32) + attn_rows.astype(F32)).astype(BF)
    mlp_in = lax.all_gather(norm_rows(middle, mlp_gain), "head", axis=0, tiled=True)
    gate, up = (dot(mlp_in, lax.all_gather(w, "group", axis=0, tiled=True)) for w in (w_gate, w_up))
    hidden = (jax.nn.silu(gate) * up).astype(BF)
    down_terms = dot(hidden, lax.all_gather(w_down, "group", axis=1, tiled=True))
    mlp_rows = lax.psum_scatter(down_terms.astype(BF), "head", scatter_dimension=0, tiled=True)
    layer_out = (middle.astype(F32) + mlp_rows.astype(F32)).astype(BF)
    return (layer_out, cache_keys, cache_values)


def octet_plan(n_group):
    octets = [[OCT * i + j for j in range(OCT)] for i in range(n_group // OCT)]
    swap = [(g, g ^ OCT) for g in range(n_group)]

    def across(x):
        return lax.ppermute(x, "group", swap)

    def other_head(x):
        return lax.ppermute(x, "head", [(0, 1), (1, 0)])

    def gather(w, axis):
        return lax.all_gather(w, "group", axis=axis, tiled=True, axis_index_groups=octets)

    def split_sum(x):
        high = x.astype(BF)
        low = (x - high.astype(F32)).astype(BF)
        return jnp.concatenate([high, low, jnp.zeros((x.shape[0], 126), BF)], axis=1)

    def exchange(partial, squares):
        rows = partial.shape[0] // 2
        sent = jnp.concatenate([partial[rows:].astype(BF), split_sum(squares[rows:])], axis=1)
        got = across(sent).astype(F32)
        width = partial.shape[1]
        total = partial[:rows] + got[:, :width]
        return total, squares[:rows] + got[:, width : width + 1] + got[:, width + 1 : width + 2]

    def per_device(
        tokens, attn_gain, w_query, w_key, w_value, w_out, mlp_gain, w_gate, w_up, w_down, segment_ids, cache_slot,
    ):
        side = lax.axis_index("group") // OCT
        row = lax.axis_index("head")
        mine, model = tokens.shape
        half = model // 2
        width = w_query.shape[1]
        units = w_gate.shape[1]

        w_qkv = gather(jnp.concatenate([w_query, w_key, w_value], axis=1), 0)
        w_o = gather(w_out, 1)
        w_gu = gather(jnp.concatenate([w_gate, w_up], axis=1), 0)
        w_d = gather(w_down, 1)

        kept = lax.dynamic_slice(tokens, (0, side * half), (mine, half))
        given = lax.dynamic_slice(tokens, (0, (1 - side) * half), (mine, half))
        both = jnp.stack([kept, across(given)])
        others = other_head(both)
        rows = jnp.stack([jnp.where(row == 0, both, others), jnp.where(row == 0, others, both)], axis=1)
        rows = rows.reshape(4 * mine, half)

        def scaled(x, gain):
            values = x.astype(F32)
            own = lax.dynamic_slice(gain, (side * half,), (half,))
            return (values * own).astype(BF), jnp.sum(values * values, axis=-1, keepdims=True)

        lhs, squares = scaled(rows, attn_gain)
        qkv, squares = exchange(dot(lhs, w_qkv), squares)
        qkv = qkv * lax.rsqrt(squares / model + EPS)
        attended, cache_keys, cache_values = attention(
            qkv[:, :width], qkv[:, width : 2 * width], qkv[:, 2 * width :].astype(BF),
            segment_ids[0], cache_slot[0],
        )
        attended = jnp.concatenate([attended, across(attended)], axis=0)
        terms = dot(attended, w_o).astype(BF)
        middle = (rows.astype(F32) + (terms.astype(F32) + other_head(terms).astype(F32))).astype(BF)
        lhs, squares = scaled(middle, mlp_gain)
        gu, squares = exchange(dot(lhs, w_gu), squares)
        gu = gu * lax.rsqrt(squares / model + EPS)
        hidden = (jax.nn.silu(gu[:, :units]) * gu[:, units:]).astype(BF)
        hidden = jnp.concatenate([hidden, across(hidden)], axis=0)
        terms = dot(hidden, w_d).astype(BF).reshape(2, 2, mine, half)
        given = other_head(lax.dynamic_index_in_dim(terms, 1 - row, 1, keepdims=False))
        mlp = lax.dynamic_index_in_dim(terms, row, 1, keepdims=False).astype(F32) + given.astype(F32)
        kept = lax.dynamic_index_in_dim(middle.reshape(2, 2, mine, half), row, 1, keepdims=False)
        out = (kept.astype(F32) + mlp).astype(BF)
        got = across(out[1])
        layer_out = jnp.where(
            side == 0, jnp.concatenate([out[0], got], axis=1), jnp.concatenate([got, out[0]], axis=1)
        )
        return (layer_out, cache_keys, cache_values)

    return per_device


def solution(mesh):
    n_group = mesh.shape["group"]
    in_specs = (
        P(("group", "head"), None),
        P(),
        P("group", "head"),
        P("group", "head"),
        P("group", "head"),
        P("head", "group"),
        P(),
        P("group", "head"),
        P("group", "head"),
        P("head", "group"),
        P("group", None),
        P("group", None),
    )
    out_specs = (P(("group", "head"), None), P("group", "head"), P("group", "head"))
    body = octet_plan(n_group) if n_group == 2 * OCT else gathered_plan
    return jax.shard_map(body, mesh=mesh, in_specs=in_specs, out_specs=out_specs, check_vma=False)
```

```python
import functools

import jax
import jax.numpy as jnp
from jax import lax
from jax.experimental import pallas as pl
from jax.experimental.pallas import tpu as pltpu
from jax.sharding import PartitionSpec as P

HEAD_DIM = 96
EPS = 1e-05
OCT = 8
BF = jnp.bfloat16
F32 = jnp.float32
VMEM = 32 * 1024 * 1024
VMEM_ALL = 60 * 1024 * 1024


def norm_rows(rows, gain):
    values = rows.astype(F32)
    scale = lax.rsqrt(jnp.mean(values * values, axis=-1, keepdims=True) + EPS)
    return (values * scale * gain).astype(BF)


def positions(segment):
    count = segment.shape[0]
    index = jnp.arange(count, dtype=jnp.int32)
    before = jnp.concatenate([jnp.full((1,), -1, jnp.int32), segment[:-1]])
    starts = jnp.where(segment != before, index, jnp.zeros_like(index))
    return index - lax.cummax(starts, axis=0)


def rotate(heads, place):
    half = heads.shape[-1] // 2
    freq = 10000.0 ** (-2.0 * jnp.arange(half, dtype=F32) / heads.shape[-1])
    angle = place.astype(F32)[:, None] * freq[None, :]
    cosine = jnp.cos(angle)[:, None, :]
    sine = jnp.sin(angle)[:, None, :]
    first = heads[..., :half]
    second = heads[..., half:]
    return jnp.concatenate(
        [first * cosine - second * sine, second * cosine + first * sine], axis=-1
    )


def dot(a, b):
    return jnp.dot(a, b, preferred_element_type=F32)


def attention(query, key, v_b, segment, slots):
    count, width = v_b.shape
    heads_here = width // HEAD_DIM
    index = jnp.arange(count, dtype=jnp.int32)
    place = positions(segment)
    q_rot = rotate(query.reshape(count, heads_here, HEAD_DIM), place).astype(BF)
    k_rot = rotate(key.reshape(count, heads_here, HEAD_DIM), place).astype(BF)
    k_flat = k_rot.reshape(count, width)
    cache_keys = jnp.zeros_like(k_flat).at[slots].set(k_flat)
    cache_values = jnp.zeros_like(v_b).at[slots].set(v_b)
    allowed = (segment[:, None] == segment[None, :]) & (index[None, :] <= index[:, None])
    scores = jnp.einsum("qhd,khd->hqk", q_rot, k_rot, preferred_element_type=F32)
    scores = scores * (1.0 / HEAD_DIM**0.5)
    scores = jnp.where(allowed[None, :, :], scores, -1e30)
    top = jnp.max(scores, axis=-1, keepdims=True)
    expo = jnp.exp(scores - top)
    probs = (expo / jnp.sum(expo, axis=-1, keepdims=True)).astype(BF)
    v_heads = v_b.reshape(count, heads_here, HEAD_DIM)
    attended = jnp.einsum("hqk,khd->qhd", probs, v_heads, preferred_element_type=F32)
    return attended.astype(BF).reshape(count, width), cache_keys, cache_values


def gathered_plan(
    tokens, attn_gain, w_query, w_key, w_value, w_out, mlp_gain, w_gate, w_up, w_down, segment_ids, cache_slot,
):
    whole = lax.all_gather(norm_rows(tokens, attn_gain), "head", axis=0, tiled=True)
    query, key, value = (
        dot(whole, lax.all_gather(w, "group", axis=0, tiled=True)) for w in (w_query, w_key, w_value)
    )
    attended, cache_keys, cache_values = attention(
        query, key, value.astype(BF), segment_ids[0], cache_slot[0]
    )
    out_terms = dot(attended, lax.all_gather(w_out, "group", axis=1, tiled=True))
    attn_rows = lax.psum_scatter(out_terms.astype(BF), "head", scatter_dimension=0, tiled=True)
    middle = (tokens.astype(F32) + attn_rows.astype(F32)).astype(BF)
    mlp_in = lax.all_gather(norm_rows(middle, mlp_gain), "head", axis=0, tiled=True)
    gate, up = (dot(mlp_in, lax.all_gather(w, "group", axis=0, tiled=True)) for w in (w_gate, w_up))
    hidden = (jax.nn.silu(gate) * up).astype(BF)
    down_terms = dot(hidden, lax.all_gather(w_down, "group", axis=1, tiled=True))
    mlp_rows = lax.psum_scatter(down_terms.astype(BF), "head", scatter_dimension=0, tiled=True)
    layer_out = (middle.astype(F32) + mlp_rows.astype(F32)).astype(BF)
    return (layer_out, cache_keys, cache_values)


def prepared(x, gain_ref, lhs_ref, coded_ref, squares_ref):
    rows, depth = x.shape
    keep, wide = rows // 2, depth // OCT
    squares = jnp.broadcast_to(jnp.sum(x * x, axis=1, keepdims=True), (rows, 128))
    scaled = (x * gain_ref[...]).astype(BF)
    if len(lhs_ref.shape) == 2:
        lhs_ref[...] = scaled
    else:
        for i in range(OCT):
            lhs_ref[i] = scaled[:, i * wide : (i + 1) * wide]
    high = squares.astype(BF).astype(F32)
    lane = lax.broadcasted_iota(jnp.int32, (rows, 128), 1)
    coded_ref[...] = jnp.where(lane < 64, high, squares - high)[keep:].astype(BF)
    squares_ref[...] = squares[:keep]


def first_kernel(row, kept_ref, partner_ref, others_ref, gain_ref, rows_ref, lhs_ref, coded_ref, squares_ref):
    mine = kept_ref.shape[0]
    own = (kept_ref, partner_ref)
    for g in range(2):
        at = pl.multiple_of(2 * mine * g + row[0] * mine, mine)
        rows_ref[pl.ds(at, mine)] = own[g][...]
        at = pl.multiple_of(2 * mine * g + (1 - row[0]) * mine, mine)
        rows_ref[pl.ds(at, mine)] = others_ref[g]
    prepared(rows_ref[...].astype(F32), gain_ref, lhs_ref, coded_ref, squares_ref)


def middle_kernel(row, rows_ref, terms_ref, others_ref, gain_ref, middle_ref, lhs_ref, coded_ref, squares_ref):
    total = terms_ref[...].astype(F32) + others_ref[...].astype(F32)
    middle_ref[...] = (rows_ref[...].astype(F32) + total).astype(BF)
    prepared(middle_ref[...].astype(F32), gain_ref, lhs_ref, coded_ref, squares_ref)


def prepare(kernel, row, operands, rows, depth, cut):
    keep = rows // 2
    shapes = [
        jax.ShapeDtypeStruct((rows, depth), BF),
        jax.ShapeDtypeStruct((OCT, rows, depth // OCT) if cut else (rows, depth), BF),
        jax.ShapeDtypeStruct((keep, 128), BF),
        jax.ShapeDtypeStruct((keep, 128), F32),
    ]
    def spec(x):
        return pl.BlockSpec(x.shape, lambda j, p: (0,) * len(x.shape))
    return pl.pallas_call(
        kernel,
        grid_spec=pltpu.PrefetchScalarGridSpec(
            num_scalar_prefetch=1,
            grid=(1,),
            in_specs=[spec(x) for x in operands],
            out_specs=[spec(x) for x in shapes],
        ),
        out_shape=shapes,
        compiler_params=pltpu.CompilerParams(vmem_limit_bytes=VMEM),
    )(row, *operands)


def rows_kernel(place, lhs, coded_ref, *refs):
    weights, (sent_ref, own_ref) = refs[: 2 * OCT], refs[2 * OCT :]
    step = pl.program_id(0)
    block = weights[0].shape[-1]
    keep, width = own_ref.shape

    @pl.when(step == 0)
    def _():
        sent_ref[:, width:] = coded_ref[...]

    for i in range(2):
        total = None
        for k in range(OCT):
            term = dot(lhs[place[0] ^ k], weights[OCT * i + k][...])
            total = term if total is None else total + term
        columns = pl.ds(pl.multiple_of(i * (width // 2) + step * block, 128), block)
        own_ref[:, columns] = total[:keep]
        sent_ref[:, columns] = total[keep:].astype(BF)


def rows_product(place, lhs, coded, pieces, block):
    _, rows, wide = lhs.shape
    keep = rows // 2
    each = pieces[0].shape[1]
    width = 2 * each
    whole = lambda j, p: (0, 0)
    return pl.pallas_call(
        rows_kernel,
        grid_spec=pltpu.PrefetchScalarGridSpec(
            num_scalar_prefetch=1,
            grid=(each // block,),
            in_specs=[pl.BlockSpec(lhs.shape, lambda j, p: (0, 0, 0)), pl.BlockSpec(coded.shape, whole)]
            + [pl.BlockSpec((wide, block), lambda j, p: (0, j))] * len(pieces),
            out_specs=[pl.BlockSpec((keep, width + 128), whole), pl.BlockSpec((keep, width), whole)],
        ),
        out_shape=[jax.ShapeDtypeStruct((keep, width + 128), BF), jax.ShapeDtypeStruct((keep, width), F32)],
        compiler_params=pltpu.CompilerParams(vmem_limit_bytes=VMEM_ALL),
    )(place, lhs, coded, *pieces)


def flat_kernel(x_ref, coded_ref, w_ref, sent_ref, own_ref):
    step = pl.program_id(0)
    block = w_ref.shape[1]
    keep, width = own_ref.shape
    if sent_ref.shape[1] > width:

        @pl.when(step == 0)
        def _():
            sent_ref[:, width:] = coded_ref[...]

    total = dot(x_ref[...], w_ref[...])
    columns = pl.ds(pl.multiple_of(step * block, 128), block)
    own_ref[:, columns] = total[:keep]
    sent_ref[:, columns] = total[keep:].astype(BF)


def flat_product(x, coded, w, block, with_squares):
    rows, depth = x.shape
    keep = rows // 2
    width = w.shape[1]
    sent = width + (128 if with_squares else 0)
    whole = lambda j: (0, 0)
    return pl.pallas_call(
        flat_kernel,
        grid=(width // block,),
        in_specs=[
            pl.BlockSpec(x.shape, whole),
            pl.BlockSpec(coded.shape, whole),
            pl.BlockSpec((depth, block), lambda j: (0, j)),
        ],
        out_specs=[pl.BlockSpec((keep, sent), whole), pl.BlockSpec((keep, width), whole)],
        out_shape=[jax.ShapeDtypeStruct((keep, sent), BF), jax.ShapeDtypeStruct((keep, width), F32)],
        compiler_params=pltpu.CompilerParams(vmem_limit_bytes=VMEM),
    )(x, coded, w)


def columns_kernel(natural, place, own_ref, got_ref, *refs):
    weights, (out_ref, parts, a_ref) = refs[:OCT], refs[OCT:]
    keep, depth = own_ref.shape
    wide = weights[0].shape[-1] // 2
    a_ref[:keep] = own_ref[...]
    a_ref[keep:] = got_ref[...]
    for k in range(OCT):
        lower = dot(a_ref[:, : depth // 2], weights[k][...])
        upper = dot(a_ref[:, depth // 2 :], weights[k][...])
        parts[k if natural else place[0] ^ k] = (lower[:, :wide] + upper[:, wide:]).astype(BF)
    for i in range(OCT):
        out_ref[:, i * wide : (i + 1) * wide] = parts[i]


def columns_product(place, own, got, pieces):
    keep, depth = own.shape
    rows = 2 * keep
    natural = len(pieces) == 1
    deep, double = depth // 2, pieces[0].shape[1]
    wide = double // 2
    whole = lambda j, p: (0, 0)
    if natural:
        pieces = pieces * OCT
        specs = [pl.BlockSpec((deep, double), lambda j, p, k=k: (k, 0)) for k in range(OCT)]
    else:
        specs = [pl.BlockSpec((deep, double), whole)] * OCT
    return pl.pallas_call(
        functools.partial(columns_kernel, natural),
        grid_spec=pltpu.PrefetchScalarGridSpec(
            num_scalar_prefetch=1,
            grid=(1,),
            in_specs=[pl.BlockSpec((keep, depth), whole)] * 2 + specs,
            out_specs=pl.BlockSpec((rows, OCT * wide), whole),
            scratch_shapes=[pltpu.VMEM((OCT, rows, wide), BF), pltpu.VMEM((rows, depth), BF)],
        ),
        out_shape=jax.ShapeDtypeStruct((rows, OCT * wide), BF),
        compiler_params=pltpu.CompilerParams(vmem_limit_bytes=VMEM),
    )(place, own, got, *pieces)


def attention_kernel(model, *refs):
    own, got, squares, cosine, left, right, seg_row, seg_col, slot, out_ref, keys_ref, values_ref = refs
    count, width = out_ref.shape
    heads_here = width // HEAD_DIM
    last = got[:, 3 * width :].astype(F32)
    scale = lax.rsqrt((squares[:, :1] + last[:, :1] + last[:, 64:65]) / model + EPS)
    query, key, value = (
        (own[:, i * width : (i + 1) * width] + got[:, i * width : (i + 1) * width].astype(F32)) * scale for i in range(3)
    )

    def rotated(x):
        ahead = pltpu.roll(x, width - HEAD_DIM // 2, 1)
        behind = pltpu.roll(x, HEAD_DIM // 2, 1)
        return (x * cosine[...] + ahead * left[...] + behind * right[...]).astype(BF)

    q_rot, k_rot, v_b = rotated(query), rotated(key), value.astype(BF)
    spot = lax.broadcasted_iota(jnp.int32, (count, count), 0)
    hot = jnp.where(spot == slot[...], 1.0, 0.0).astype(BF)
    keys_ref[...] = dot(hot, k_rot).astype(BF)
    values_ref[...] = dot(hot, v_b).astype(BF)
    lane = lax.broadcasted_iota(jnp.int32, (count, width), 1)
    within = [(lane >= h * HEAD_DIM) & (lane < (h + 1) * HEAD_DIM) for h in range(heads_here)]
    zero = jnp.zeros((count, width), BF)
    spread_q = jnp.concatenate([jnp.where(w, q_rot, zero) for w in within], axis=0)
    scores = lax.dot_general(spread_q, k_rot, (((1,), (1,)), ((), ())), preferred_element_type=F32)
    scores = (scores * (1.0 / HEAD_DIM**0.5)).reshape(heads_here, count, count)
    other = lax.broadcasted_iota(jnp.int32, (count, count), 1)
    allowed = (seg_col[...] == seg_row[...]) & (other <= spot)
    scores = jnp.where(allowed[None], scores, -1e30)
    expo = jnp.exp(scores - jnp.max(scores, axis=-1, keepdims=True))
    probs = (expo / jnp.sum(expo, axis=-1, keepdims=True)).astype(BF)
    mixed = dot(probs.reshape(heads_here * count, count), v_b)
    total = jnp.zeros((count, width), F32)
    for h in range(heads_here):
        total = total + jnp.where(within[h], mixed[h * count : (h + 1) * count], 0.0)
    out_ref[...] = total.astype(BF)


def attend(model, own, got, squares, tables, segment, slots):
    count, width = own.shape[0], own.shape[1] // 3
    out = jax.ShapeDtypeStruct((count, width), BF)
    return pl.pallas_call(
        functools.partial(attention_kernel, model),
        out_shape=[out, out, out],
        compiler_params=pltpu.CompilerParams(vmem_limit_bytes=VMEM),
    )(own, got, squares, *tables, segment.reshape(1, count), segment.reshape(count, 1), slots.reshape(1, count))


def rotation_tables(segment, width):
    half = HEAD_DIM // 2
    lane = jnp.arange(width, dtype=jnp.int32)
    freq = 10000.0 ** (-2.0 * (lane % half).astype(F32) / HEAD_DIM)
    angle = positions(segment).astype(F32)[:, None] * freq[None, :]
    first = ((lane % HEAD_DIM) < half)[None, :]
    sine = jnp.sin(angle)
    return jnp.cos(angle), jnp.where(first, -sine, 0.0), jnp.where(first, 0.0, sine)


def after(x, *others):
    return lax.optimization_barrier((x,) + others)[0]


def octet_plan(n_group):
    def swap(bit):
        pairs = [(g, g ^ bit) for g in range(n_group)]
        return lambda x: lax.ppermute(x, "group", pairs)

    octets = [[OCT * i + j for j in range(OCT)] for i in range(n_group // OCT)]
    core, near, next_to, across = swap(1), swap(2), swap(4), swap(OCT)

    def other_head(x):
        return lax.ppermute(x, "head", [(0, 1), (1, 0)])

    def beside(w):
        depth = w.shape[0]
        return jnp.concatenate([w[: depth // 2], w[depth // 2 :]], axis=1)

    def all_pieces(own, x, z, diagonal):
        return [p for part in (own, x, z, diagonal) for p in (part, core(part))]

    def gathered(w):
        return lax.all_gather(w, "group", axis=0, tiled=True, axis_index_groups=octets)

    def per_device(
        tokens, attn_gain, w_query, w_key, w_value, w_out, mlp_gain, w_gate, w_up, w_down, segment_ids, cache_slot,
    ):
        group = lax.axis_index("group")
        side = group // OCT
        place = (group % OCT).astype(jnp.int32).reshape(1)
        row = lax.axis_index("head")
        at_row = row.astype(jnp.int32).reshape(1)
        mine, model = tokens.shape
        half = model // 2
        width = w_query.shape[1]
        units = w_gate.shape[1]

        def own_gain(gain):
            return lax.dynamic_slice(gain, (side * half,), (half,)).reshape(1, half)

        kept = lax.dynamic_slice(tokens, (0, side * half), (mine, half))
        given = lax.dynamic_slice(tokens, (0, (1 - side) * half), (mine, half))
        gain1, gain2 = own_gain(attn_gain), own_gain(mlp_gain)
        o_own, d_own = lax.optimization_barrier((beside(w_out), beside(w_down)))
        tables = rotation_tables(segment_ids[0], width)
        w_g, w_u, w_d = gathered(w_gate), gathered(w_up), gathered(d_own)
        partner = across(given)
        cut = width // 2
        first = jnp.concatenate([w_query, w_key[:, :cut]], axis=1)
        second = jnp.concatenate([w_key[:, cut:], w_value], axis=1)
        x_1, x_2 = near(first), near(second)
        z_2, z_1 = next_to(second), next_to(first)
        others = other_head(jnp.stack([kept, partner]))
        d_1, d_2 = next_to(after(x_1, others)), near(z_2)
        x_o, z_o = near(after(o_own, d_1)), next_to(after(o_own, d_1))
        d_o = near(z_o)
        others = after(others, gain1, gain2, *tables)
        rows, lhs, coded, squares = prepare(
            first_kernel, at_row, (kept, partner, others, gain1), 4 * mine, half, True
        )
        pieces = all_pieces(first, x_1, z_1, d_1) + all_pieces(second, x_2, z_2, d_2)
        sent, own = rows_product(place, lhs, coded, pieces, 384)
        got = after(across(sent), x_o, z_o)
        attended, cache_keys, cache_values = attend(model, own, got, squares, tables, segment_ids[0], cache_slot[0])
        terms = columns_product(place, attended, across(attended), all_pieces(o_own, x_o, z_o, d_o))
        middle, lhs, coded, squares = prepare(
            middle_kernel, at_row, (rows, terms, other_head(terms), gain2), 4 * mine, half, False
        )
        sent_g, own_g = flat_product(lhs, coded, w_g, 512, True)
        got_g = across(sent_g)
        sent_u, own_u = flat_product(after(lhs, sent_g), coded, w_u, 512, False)
        got_u = across(sent_u)
        last = got_g[:, units:].astype(F32)
        scale = lax.rsqrt((squares[:, :1] + last[:, :1] + last[:, 64:65]) / model + EPS)
        gate = (own_g + got_g[:, :units].astype(F32)) * scale
        up = (own_u + got_u.astype(F32)) * scale
        hidden = (jax.nn.silu(gate) * up).astype(BF)
        terms = columns_product(place, hidden, across(hidden), [w_d]).reshape(2, 2, mine, half)
        given = other_head(lax.dynamic_index_in_dim(terms, 1 - row, 1, keepdims=False))
        mlp = lax.dynamic_index_in_dim(terms, row, 1, keepdims=False).astype(F32) + given.astype(F32)
        kept = lax.dynamic_index_in_dim(middle.reshape(2, 2, mine, half), row, 1, keepdims=False)
        out = (kept.astype(F32) + mlp).astype(BF)
        got = across(out[1])
        layer_out = jnp.where(
            side == 0, jnp.concatenate([out[0], got], axis=1), jnp.concatenate([got, out[0]], axis=1)
        )
        return (layer_out, cache_keys, cache_values)

    return per_device


def solution(mesh):
    n_group = mesh.shape["group"]
    in_specs = (
        P(("group", "head"), None),
        P(),
        P("group", "head"),
        P("group", "head"),
        P("group", "head"),
        P("head", "group"),
        P(),
        P("group", "head"),
        P("group", "head"),
        P("head", "group"),
        P("group", None),
        P("group", None),
    )
    out_specs = (P(("group", "head"), None), P("group", "head"), P("group", "head"))
    body = octet_plan(n_group) if n_group == 2 * OCT else gathered_plan
    return jax.shard_map(body, mesh=mesh, in_specs=in_specs, out_specs=out_specs, check_vma=False)
```

```python
import functools

import jax
import jax.numpy as jnp
from jax import lax
from jax.experimental import pallas as pl
from jax.experimental.pallas import tpu as pltpu
from jax.sharding import PartitionSpec as P

HEAD_DIM = 96
EPS = 1e-05
OCT = 8
QUAD = 4
BF = jnp.bfloat16
F32 = jnp.float32
VMEM = 24 * 1024 * 1024
VMEM_ALL = 60 * 1024 * 1024


def norm_rows(rows, gain):
    values = rows.astype(F32)
    scale = lax.rsqrt(jnp.mean(values * values, axis=-1, keepdims=True) + EPS)
    return (values * scale * gain).astype(BF)


def positions(segment):
    count = segment.shape[0]
    index = jnp.arange(count, dtype=jnp.int32)
    before = jnp.concatenate([jnp.full((1,), -1, jnp.int32), segment[:-1]])
    starts = jnp.where(segment != before, index, jnp.zeros_like(index))
    return index - lax.cummax(starts, axis=0)


def rotate(heads, place):
    half = heads.shape[-1] // 2
    freq = 10000.0 ** (-2.0 * jnp.arange(half, dtype=F32) / heads.shape[-1])
    angle = place.astype(F32)[:, None] * freq[None, :]
    cosine = jnp.cos(angle)[:, None, :]
    sine = jnp.sin(angle)[:, None, :]
    first = heads[..., :half]
    second = heads[..., half:]
    return jnp.concatenate(
        [first * cosine - second * sine, second * cosine + first * sine], axis=-1
    )


def dot(a, b):
    return jnp.dot(a, b, preferred_element_type=F32)


def attention(query, key, v_b, segment, slots):
    count, width = v_b.shape
    heads_here = width // HEAD_DIM
    index = jnp.arange(count, dtype=jnp.int32)
    place = positions(segment)
    q_rot = rotate(query.reshape(count, heads_here, HEAD_DIM), place).astype(BF)
    k_rot = rotate(key.reshape(count, heads_here, HEAD_DIM), place).astype(BF)
    k_flat = k_rot.reshape(count, width)
    cache_keys = jnp.zeros_like(k_flat).at[slots].set(k_flat)
    cache_values = jnp.zeros_like(v_b).at[slots].set(v_b)
    allowed = (segment[:, None] == segment[None, :]) & (index[None, :] <= index[:, None])
    scores = jnp.einsum("qhd,khd->hqk", q_rot, k_rot, preferred_element_type=F32)
    scores = scores * (1.0 / HEAD_DIM**0.5)
    scores = jnp.where(allowed[None, :, :], scores, -1e30)
    top = jnp.max(scores, axis=-1, keepdims=True)
    expo = jnp.exp(scores - top)
    probs = (expo / jnp.sum(expo, axis=-1, keepdims=True)).astype(BF)
    v_heads = v_b.reshape(count, heads_here, HEAD_DIM)
    attended = jnp.einsum("hqk,khd->qhd", probs, v_heads, preferred_element_type=F32)
    return attended.astype(BF).reshape(count, width), cache_keys, cache_values


def gathered_plan(
    tokens, attn_gain, w_query, w_key, w_value, w_out, mlp_gain, w_gate, w_up, w_down, segment_ids, cache_slot,
):
    whole = lax.all_gather(norm_rows(tokens, attn_gain), "head", axis=0, tiled=True)
    query, key, value = (
        dot(whole, lax.all_gather(w, "group", axis=0, tiled=True)) for w in (w_query, w_key, w_value)
    )
    attended, cache_keys, cache_values = attention(
        query, key, value.astype(BF), segment_ids[0], cache_slot[0]
    )
    out_terms = dot(attended, lax.all_gather(w_out, "group", axis=1, tiled=True))
    attn_rows = lax.psum_scatter(out_terms.astype(BF), "head", scatter_dimension=0, tiled=True)
    middle = (tokens.astype(F32) + attn_rows.astype(F32)).astype(BF)
    mlp_in = lax.all_gather(norm_rows(middle, mlp_gain), "head", axis=0, tiled=True)
    gate, up = (dot(mlp_in, lax.all_gather(w, "group", axis=0, tiled=True)) for w in (w_gate, w_up))
    hidden = (jax.nn.silu(gate) * up).astype(BF)
    down_terms = dot(hidden, lax.all_gather(w_down, "group", axis=1, tiled=True))
    mlp_rows = lax.psum_scatter(down_terms.astype(BF), "head", scatter_dimension=0, tiled=True)
    layer_out = (middle.astype(F32) + mlp_rows.astype(F32)).astype(BF)
    return (layer_out, cache_keys, cache_values)


def prepared(x, keep, gain_ref, lhs_ref, coded_ref, squares_ref):
    rows, depth = x.shape
    cuts = lhs_ref.shape[0]
    wide = depth // cuts
    squares = jnp.broadcast_to(jnp.sum(x * x, axis=1, keepdims=True), (rows, 128))
    scaled = (x * gain_ref[...]).astype(BF)
    for i in range(cuts):
        lhs_ref[i] = scaled[:, i * wide : (i + 1) * wide]
    high = squares.astype(BF).astype(F32)
    lane = lax.broadcasted_iota(jnp.int32, (rows, 128), 1)
    coded_ref[...] = jnp.where(lane < 64, high, squares - high)[keep:].astype(BF)
    squares_ref[...] = squares[:keep]


def arranged(row, rows_ref, mine_ref, others_ref):
    groups, mine, _ = mine_ref.shape
    for g in range(groups):
        rows_ref[pl.ds(pl.multiple_of(2 * mine * g + row[0] * mine, mine), mine)] = mine_ref[g]
        rows_ref[pl.ds(pl.multiple_of(2 * mine * g + (1 - row[0]) * mine, mine), mine)] = others_ref[g]


def first_kernel(row, mine_ref, others_ref, gain_ref, rows_ref, lhs_ref, coded_ref, squares_ref):
    arranged(row, rows_ref, mine_ref, others_ref)
    prepared(rows_ref[...].astype(F32), squares_ref.shape[0], gain_ref, lhs_ref, coded_ref, squares_ref)


def middle_kernel(row, mine_ref, others_ref, a_ref, b_ref, gain_ref, middle_ref, lhs_ref, coded_ref, squares_ref):
    arranged(row, middle_ref, mine_ref, others_ref)
    total = a_ref[...].astype(F32) + b_ref[...].astype(F32)
    middle_ref[...] = (middle_ref[...].astype(F32) + total).astype(BF)
    prepared(middle_ref[...].astype(F32), squares_ref.shape[0], gain_ref, lhs_ref, coded_ref, squares_ref)


def prepare(kernel, row, operands, rows, depth, keep, cuts):
    shapes = [
        jax.ShapeDtypeStruct((rows, depth), BF),
        jax.ShapeDtypeStruct((cuts, rows, depth // cuts), BF),
        jax.ShapeDtypeStruct((rows - keep, 128), BF),
        jax.ShapeDtypeStruct((keep, 128), F32),
    ]
    def spec(x):
        return pl.BlockSpec(x.shape, lambda j, p: (0,) * len(x.shape))
    return pl.pallas_call(
        kernel,
        grid_spec=pltpu.PrefetchScalarGridSpec(
            num_scalar_prefetch=1,
            grid=(1,),
            in_specs=[spec(x) for x in operands],
            out_specs=[spec(x) for x in shapes],
        ),
        out_shape=shapes,
        compiler_params=pltpu.CompilerParams(vmem_limit_bytes=VMEM),
    )(row, *operands)


def rows_kernel(place, lhs, coded_ref, *refs):
    weights, (sent_ref, own_ref, held, sems) = refs[:-4], refs[-4:]
    block = held.shape[-1]
    keep, width = own_ref.shape
    parts = len(weights) // OCT
    steps = width // parts // block

    def copies(step):
        return [
            pltpu.make_async_copy(
                w.at[:, step * block : (step + 1) * block], held.at[step % 2, n], sems.at[step % 2, n]
            )
            for n, w in enumerate(weights)
        ]

    pending = copies(0)
    for c in pending:
        c.start()
    if sent_ref.shape[1] > width:
        sent_ref[:, width:] = coded_ref[...]
    for step in range(steps):
        following = copies(step + 1) if step + 1 < steps else []
        for c in following:
            c.start()
        for i in range(parts):
            total = None
            for k in range(OCT):
                pending[OCT * i + k].wait()
                term = dot(lhs[place[0] ^ k], held[step % 2, OCT * i + k])
                total = term if total is None else total + term
            at = i * (width // parts) + step * block
            own_ref[:, at : at + block] = total[:keep]
            sent_ref[:, at : at + block] = total[keep:].astype(BF)
        pending = following


def in_hbm(pieces):
    return [pl.BlockSpec(memory_space=pltpu.HBM)] * len(pieces)


def rows_product(place, lhs, coded, pieces, each, block, with_squares):
    _, rows, wide = lhs.shape
    keep = rows // 2
    count = len(pieces)
    width = count // OCT * each
    sent = width + (128 if with_squares else 0)
    whole = lambda j, p: (0, 0)
    return pl.pallas_call(
        rows_kernel,
        grid_spec=pltpu.PrefetchScalarGridSpec(
            num_scalar_prefetch=1,
            grid=(1,),
            in_specs=[pl.BlockSpec(lhs.shape, lambda j, p: (0, 0, 0)), pl.BlockSpec(coded.shape, whole)]
            + in_hbm(pieces),
            out_specs=[pl.BlockSpec((keep, sent), whole), pl.BlockSpec((keep, width), whole)],
            scratch_shapes=[pltpu.VMEM((2, count, wide, block), BF), pltpu.SemaphoreType.DMA((2, count))],
        ),
        out_shape=[jax.ShapeDtypeStruct((keep, sent), BF), jax.ShapeDtypeStruct((keep, width), F32)],
        compiler_params=pltpu.CompilerParams(vmem_limit_bytes=VMEM),
    )(place, lhs, coded, *pieces)


def first_rows_kernel(place, lhs, coded_ref, *refs):
    weights, sent_refs, own_ref = refs[:12], refs[12:15], refs[15]
    step = pl.program_id(0)
    block = weights[0].shape[-1]
    keep, width = own_ref.shape

    @pl.when(step == 0)
    def _():
        for g, sent_ref in enumerate(sent_refs):
            sent_ref[:, width:] = coded_ref[g * keep : (g + 1) * keep]

    for i in range(3):
        total = None
        for k in range(4):
            term = dot(lhs[place[0] ^ k], weights[4 * i + k][...])
            total = term if total is None else total + term
        columns = pl.ds(pl.multiple_of(i * (width // 3) + step * block, 128), block)
        own_ref[:, columns] = total[:keep]
        for g, sent_ref in enumerate(sent_refs):
            sent_ref[:, columns] = total[(g + 1) * keep : (g + 2) * keep].astype(BF)


def first_rows_product(place, lhs, coded, pieces, block):
    _, rows, wide = lhs.shape
    keep = rows // 4
    each = pieces[0].shape[1]
    width = 3 * each
    whole = lambda j, p: (0, 0)
    sent = jax.ShapeDtypeStruct((keep, width + 128), BF)
    return pl.pallas_call(
        first_rows_kernel,
        grid_spec=pltpu.PrefetchScalarGridSpec(
            num_scalar_prefetch=1,
            grid=(each // block,),
            in_specs=[pl.BlockSpec(lhs.shape, lambda j, p: (0, 0, 0)), pl.BlockSpec(coded.shape, whole)]
            + [pl.BlockSpec((wide, block), lambda j, p: (0, j))] * len(pieces),
            out_specs=[pl.BlockSpec(sent.shape, whole)] * 3 + [pl.BlockSpec((keep, width), whole)],
        ),
        out_shape=[sent] * 3 + [jax.ShapeDtypeStruct((keep, width), F32)],
        compiler_params=pltpu.CompilerParams(vmem_limit_bytes=VMEM_ALL),
    )(place, lhs, coded, *pieces)


def columns_kernel(place, own_ref, got_ref, *refs):
    weights, (out_ref, parts, a_ref, held, sems) = refs[:OCT], refs[OCT:]
    keep, depth = own_ref.shape
    wide = held.shape[2] // 2
    copies = [pltpu.make_async_copy(w, held.at[n], sems.at[n]) for n, w in enumerate(weights)]
    for c in copies:
        c.start()
    a_ref[:keep] = own_ref[...]
    a_ref[keep:] = got_ref[...]
    for k in range(OCT):
        copies[k].wait()
        lower = dot(a_ref[:, : depth // 2], held[k])
        upper = dot(a_ref[:, depth // 2 :], held[k])
        parts[place[0] ^ k] = (lower[:, :wide] + upper[:, wide:]).astype(BF)
    for i in range(OCT):
        out_ref[:, i * wide : (i + 1) * wide] = parts[i]


def columns_product(place, own, got, pieces):
    keep, depth = own.shape
    rows = 2 * keep
    deep, double = pieces[0].shape
    wide = double // 2
    whole = lambda j, p: (0, 0)
    return pl.pallas_call(
        columns_kernel,
        grid_spec=pltpu.PrefetchScalarGridSpec(
            num_scalar_prefetch=1,
            grid=(1,),
            in_specs=[pl.BlockSpec((keep, depth), whole)] * 2 + in_hbm(pieces),
            out_specs=pl.BlockSpec((rows, OCT * wide), whole),
            scratch_shapes=[
                pltpu.VMEM((OCT, rows, wide), BF),
                pltpu.VMEM((rows, depth), BF),
                pltpu.VMEM((OCT, deep, double), BF),
                pltpu.SemaphoreType.DMA((OCT,)),
            ],
        ),
        out_shape=jax.ShapeDtypeStruct((rows, OCT * wide), BF),
        compiler_params=pltpu.CompilerParams(vmem_limit_bytes=VMEM),
    )(place, own, got, *pieces)


def out_kernel(place, own_ref, got_ref, *refs):
    weights, (out_ref, parts, a_ref) = refs[:OCT], refs[OCT:]
    keep, depth = own_ref.shape
    a_ref[:keep] = own_ref[...]
    a_ref[keep:] = got_ref[...]
    wide = weights[0].shape[-1] // 2
    for k in range(OCT):
        lower = dot(a_ref[:, : depth // 2], weights[k][...])
        upper = dot(a_ref[:, depth // 2 :], weights[k][...])
        parts[place[0] ^ k] = (lower[:, :wide] + upper[:, wide:]).astype(BF)
    for i in range(OCT):
        out_ref[:, i * wide : (i + 1) * wide] = parts[i]


def out_product(place, own, got, pieces):
    keep, depth = own.shape
    rows = 2 * keep
    deep, double = pieces[0].shape
    wide = double // 2
    whole = lambda j, p: (0, 0)
    return pl.pallas_call(
        out_kernel,
        grid_spec=pltpu.PrefetchScalarGridSpec(
            num_scalar_prefetch=1,
            grid=(1,),
            in_specs=[pl.BlockSpec((keep, depth), whole)] * 2 + [pl.BlockSpec((deep, double), whole)] * OCT,
            out_specs=pl.BlockSpec((rows, OCT * wide), whole),
            scratch_shapes=[pltpu.VMEM((OCT, rows, wide), BF), pltpu.VMEM((rows, depth), BF)],
        ),
        out_shape=jax.ShapeDtypeStruct((rows, OCT * wide), BF),
        compiler_params=pltpu.CompilerParams(vmem_limit_bytes=VMEM_ALL),
    )(place, own, got, *pieces)


def attention_kernel(model, *refs):
    own, *got = refs[:4]
    squares, cosine, left, right, seg_row, seg_col, slot, out_ref, keys_ref, values_ref = refs[4:]
    count, width = out_ref.shape
    heads_here = width // HEAD_DIM
    total = squares[:, :1]
    for g in got:
        last = g[:, 3 * width :].astype(F32)
        total = total + last[:, :1] + last[:, 64:65]
    scale = lax.rsqrt(total / model + EPS)

    def part(i):
        columns = slice(i * width, (i + 1) * width)
        x = own[:, columns]
        for g in got:
            x = x + g[:, columns].astype(F32)
        return x * scale

    query, key, value = part(0), part(1), part(2)

    def rotated(x):
        ahead = pltpu.roll(x, width - HEAD_DIM // 2, 1)
        behind = pltpu.roll(x, HEAD_DIM // 2, 1)
        return (x * cosine[...] + ahead * left[...] + behind * right[...]).astype(BF)

    q_rot, k_rot, v_b = rotated(query), rotated(key), value.astype(BF)
    spot = lax.broadcasted_iota(jnp.int32, (count, count), 0)
    hot = jnp.where(spot == slot[...], 1.0, 0.0).astype(BF)
    keys_ref[...] = dot(hot, k_rot).astype(BF)
    values_ref[...] = dot(hot, v_b).astype(BF)
    lane = lax.broadcasted_iota(jnp.int32, (count, width), 1)
    within = [(lane >= h * HEAD_DIM) & (lane < (h + 1) * HEAD_DIM) for h in range(heads_here)]
    zero = jnp.zeros((count, width), BF)
    spread_q = jnp.concatenate([jnp.where(w, q_rot, zero) for w in within], axis=0)
    scores = lax.dot_general(spread_q, k_rot, (((1,), (1,)), ((), ())), preferred_element_type=F32)
    scores = (scores * (1.0 / HEAD_DIM**0.5)).reshape(heads_here, count, count)
    other = lax.broadcasted_iota(jnp.int32, (count, count), 1)
    allowed = (seg_col[...] == seg_row[...]) & (other <= spot)
    scores = jnp.where(allowed[None], scores, -1e30)
    expo = jnp.exp(scores - jnp.max(scores, axis=-1, keepdims=True))
    probs = (expo / jnp.sum(expo, axis=-1, keepdims=True)).astype(BF)
    mixed = dot(probs.reshape(heads_here * count, count), v_b)
    total = jnp.zeros((count, width), F32)
    for h in range(heads_here):
        total = total + jnp.where(within[h], mixed[h * count : (h + 1) * count], 0.0)
    out_ref[...] = total.astype(BF)


def attend(model, own, got, squares, tables, segment, slots):
    count, width = own.shape[0], own.shape[1] // 3
    out = jax.ShapeDtypeStruct((count, width), BF)
    return pl.pallas_call(
        functools.partial(attention_kernel, model),
        out_shape=[out, out, out],
        compiler_params=pltpu.CompilerParams(vmem_limit_bytes=VMEM_ALL),
    )(own, *got, squares, *tables, segment.reshape(1, count), segment.reshape(count, 1), slots.reshape(1, count))


def rotation_tables(segment, width):
    half = HEAD_DIM // 2
    lane = jnp.arange(width, dtype=jnp.int32)
    freq = 10000.0 ** (-2.0 * (lane % half).astype(F32) / HEAD_DIM)
    angle = positions(segment).astype(F32)[:, None] * freq[None, :]
    first = ((lane % HEAD_DIM) < half)[None, :]
    sine = jnp.sin(angle)
    return jnp.cos(angle), jnp.where(first, -sine, 0.0), jnp.where(first, 0.0, sine)


def after(x, *others):
    return lax.optimization_barrier((x,) + others)[0]


def octet_plan(n_group):
    def swap(bit):
        pairs = [(g, g ^ bit) for g in range(n_group)]
        return lambda x: lax.ppermute(x, "group", pairs)

    core, near, next_to, across = swap(1), swap(2), swap(4), swap(OCT)

    def other_head(x):
        return lax.ppermute(x, "head", [(0, 1), (1, 0)])

    def beside(w):
        depth = w.shape[0]
        return jnp.concatenate([w[: depth // 2], w[depth // 2 :]], axis=1)

    def all_pieces(own, x, z, diagonal, early=(), late=()):
        return [
            own, core(after(own, *early)), x, core(after(x, *early)), z, core(after(z, *early)),
            diagonal, core(after(diagonal, *late)),
        ]

    def turn(k):
        pairs = [(g, (g + k * QUAD) % n_group) for g in range(n_group)]
        return lambda x: lax.ppermute(x, "group", pairs)

    turns = [turn(k) for k in range(4)]

    def per_device(
        tokens, attn_gain, w_query, w_key, w_value, w_out, mlp_gain, w_gate, w_up, w_down, segment_ids, cache_slot,
    ):
        group = lax.axis_index("group")
        side, fourth = group // OCT, group // QUAD
        place = (group % OCT).astype(jnp.int32).reshape(1)
        place4 = (group % QUAD).astype(jnp.int32).reshape(1)
        row = lax.axis_index("head")
        at_row = row.astype(jnp.int32).reshape(1)
        mine, model = tokens.shape
        half, quarter = model // 2, model // 4
        units = w_gate.shape[1]
        width = w_query.shape[1]
        tables = rotation_tables(segment_ids[0], width)
        gain1 = lax.dynamic_slice(attn_gain, (fourth * quarter,), (quarter,)).reshape(1, quarter)
        gain2 = lax.dynamic_slice(mlp_gain, (side * half,), (half,)).reshape(1, half)

        def columns_of(place, wide):
            return lax.dynamic_slice(tokens, (0, place * wide), (mine, wide))

        cut = [columns_of((fourth + k) % 4, quarter) for k in range(4)]
        given = columns_of(1 - side, half)
        cut = lax.optimization_barrier((*cut, given))
        came = [turns[k](cut[k]) for k in (3, 2, 1)]
        x_q, x_k, x_v = near(w_query), near(w_key), near(w_value)
        o_own, d_own = lax.optimization_barrier((beside(w_out), beside(w_down)))
        x_o = near(o_own)
        both = jnp.stack([cut[0], *came])
        gate, down, z_own, given = lax.optimization_barrier((w_gate, d_own, o_own, cut[4], both))[:4]
        partner = across(given)
        z_o, z_g, z_d = next_to(z_own), next_to(gate), next_to(down)
        mine_too = jnp.stack([columns_of(side, half), partner])
        others_too = other_head(mine_too)
        others = other_head(after(both, x_q, gain1, gain2, *tables, z_g, others_too))
        _, lhs, coded, squares = prepare(
            first_kernel, at_row, (both, others, gain1), 8 * mine, quarter, 2 * mine, QUAD
        )
        x_gate, x_up, x_down = lax.optimization_barrier((w_gate, w_up, d_own, x_q, x_k, x_v, x_o, both))[:3]
        x_g, x_u, x_d = near(x_gate), near(x_up), near(x_down)
        pieces = [p for w, x in ((w_query, x_q), (w_key, x_k), (w_value, x_v)) for p in (w, core(w), x, core(x))]
        *sent, own = first_rows_product(place4, after(lhs, partner), coded, pieces, 384)
        *sent, _ = lax.optimization_barrier((*sent, z_o, z_d))[:4]
        got = [turns[k + 1](sent[k]) for k in range(3)]
        d_o = near(after(z_o, sent[0]))
        got = lax.optimization_barrier((*got, d_o, x_g, x_u, x_d))[:3]
        p_o = all_pieces(o_own, x_o, z_o, d_o, (sent[0],), (sent[0],))
        attended, cache_keys, cache_values = attend(model, own, got, squares, tables, segment_ids[0], cache_slot[0])
        d_g = near(after(z_g, attended))
        got = across(attended)
        z_u = next_to(after(w_up, got))
        terms = out_product(place, attended, got, p_o)
        others = other_head(terms)
        p_g = all_pieces(w_gate, x_g, z_g, d_g, (attended,), (others,))
        middle, lhs, coded, squares = prepare(
            middle_kernel, at_row, (mine_too, others_too, terms, after(others, z_u, d_g), gain2), 4 * mine, half, 2 * mine, OCT
        )
        d_u = near(after(z_u, lhs))
        sent_g, own_g = rows_product(place, lhs, coded, p_g, units, 512, True)
        got_g = across(sent_g)
        p_u = all_pieces(w_up, x_u, z_u, d_u, (lhs,), (got_g,))
        sent_u, own_u = rows_product(place, after(lhs, sent_g), coded, p_u, units, 512, False)
        got_u = across(sent_u)
        d_d = near(after(z_d, sent_g))
        p_d = all_pieces(d_own, x_d, z_d, d_d, (sent_u,), (got_u,))
        last = got_g[:, units:].astype(F32)
        scale = lax.rsqrt((squares[:, :1] + last[:, :1] + last[:, 64:65]) / model + EPS)
        gate = (own_g + got_g[:, :units].astype(F32)) * scale
        up = (own_u + got_u.astype(F32)) * scale
        hidden = (jax.nn.silu(gate) * up).astype(BF)
        terms = columns_product(place, hidden, across(hidden), p_d).reshape(2, 2, mine, half)
        given = other_head(lax.dynamic_index_in_dim(terms, 1 - row, 1, keepdims=False))
        mlp = lax.dynamic_index_in_dim(terms, row, 1, keepdims=False).astype(F32) + given.astype(F32)
        kept = lax.dynamic_index_in_dim(middle.reshape(2, 2, mine, half), row, 1, keepdims=False)
        out = (kept.astype(F32) + mlp).astype(BF)
        got = across(out[1])
        layer_out = jnp.where(
            side == 0, jnp.concatenate([out[0], got], axis=1), jnp.concatenate([got, out[0]], axis=1)
        )
        return (layer_out, cache_keys, cache_values)

    return per_device


def solution(mesh):
    n_group = mesh.shape["group"]
    in_specs = (
        P(("group", "head"), None),
        P(),
        P("group", "head"),
        P("group", "head"),
        P("group", "head"),
        P("head", "group"),
        P(),
        P("group", "head"),
        P("group", "head"),
        P("head", "group"),
        P("group", None),
        P("group", None),
    )
    out_specs = (P(("group", "head"), None), P("group", "head"), P("group", "head"))
    body = octet_plan(n_group) if n_group == 2 * OCT else gathered_plan
    return jax.shard_map(body, mesh=mesh, in_specs=in_specs, out_specs=out_specs, check_vma=False)
```

```python
import functools

import jax
import jax.numpy as jnp
from jax import lax
from jax.experimental import pallas as pl
from jax.experimental.pallas import tpu as pltpu
from jax.sharding import PartitionSpec as P

HEAD_DIM = 96
EPS = 1e-05
OCT = 8
QUAD = 4
BF = jnp.bfloat16
F32 = jnp.float32
VMEM = 24 * 1024 * 1024
VMEM_ALL = 60 * 1024 * 1024


def norm_rows(rows, gain):
    values = rows.astype(F32)
    scale = lax.rsqrt(jnp.mean(values * values, axis=-1, keepdims=True) + EPS)
    return (values * scale * gain).astype(BF)


def positions(segment):
    count = segment.shape[0]
    index = jnp.arange(count, dtype=jnp.int32)
    before = jnp.concatenate([jnp.full((1,), -1, jnp.int32), segment[:-1]])
    starts = jnp.where(segment != before, index, jnp.zeros_like(index))
    return index - lax.cummax(starts, axis=0)


def rotate(heads, place):
    half = heads.shape[-1] // 2
    freq = 10000.0 ** (-2.0 * jnp.arange(half, dtype=F32) / heads.shape[-1])
    angle = place.astype(F32)[:, None] * freq[None, :]
    cosine = jnp.cos(angle)[:, None, :]
    sine = jnp.sin(angle)[:, None, :]
    first = heads[..., :half]
    second = heads[..., half:]
    return jnp.concatenate(
        [first * cosine - second * sine, second * cosine + first * sine], axis=-1
    )


def dot(a, b):
    return jnp.dot(a, b, preferred_element_type=F32)


def attention(query, key, v_b, segment, slots):
    count, width = v_b.shape
    heads_here = width // HEAD_DIM
    index = jnp.arange(count, dtype=jnp.int32)
    place = positions(segment)
    q_rot = rotate(query.reshape(count, heads_here, HEAD_DIM), place).astype(BF)
    k_rot = rotate(key.reshape(count, heads_here, HEAD_DIM), place).astype(BF)
    k_flat = k_rot.reshape(count, width)
    cache_keys = jnp.zeros_like(k_flat).at[slots].set(k_flat)
    cache_values = jnp.zeros_like(v_b).at[slots].set(v_b)
    allowed = (segment[:, None] == segment[None, :]) & (index[None, :] <= index[:, None])
    scores = jnp.einsum("qhd,khd->hqk", q_rot, k_rot, preferred_element_type=F32)
    scores = scores * (1.0 / HEAD_DIM**0.5)
    scores = jnp.where(allowed[None, :, :], scores, -1e30)
    top = jnp.max(scores, axis=-1, keepdims=True)
    expo = jnp.exp(scores - top)
    probs = (expo / jnp.sum(expo, axis=-1, keepdims=True)).astype(BF)
    v_heads = v_b.reshape(count, heads_here, HEAD_DIM)
    attended = jnp.einsum("hqk,khd->qhd", probs, v_heads, preferred_element_type=F32)
    return attended.astype(BF).reshape(count, width), cache_keys, cache_values


def gathered_plan(
    tokens, attn_gain, w_query, w_key, w_value, w_out, mlp_gain, w_gate, w_up, w_down, segment_ids, cache_slot,
):
    whole = lax.all_gather(norm_rows(tokens, attn_gain), "head", axis=0, tiled=True)
    query, key, value = (
        dot(whole, lax.all_gather(w, "group", axis=0, tiled=True)) for w in (w_query, w_key, w_value)
    )
    attended, cache_keys, cache_values = attention(
        query, key, value.astype(BF), segment_ids[0], cache_slot[0]
    )
    out_terms = dot(attended, lax.all_gather(w_out, "group", axis=1, tiled=True))
    attn_rows = lax.psum_scatter(out_terms.astype(BF), "head", scatter_dimension=0, tiled=True)
    middle = (tokens.astype(F32) + attn_rows.astype(F32)).astype(BF)
    mlp_in = lax.all_gather(norm_rows(middle, mlp_gain), "head", axis=0, tiled=True)
    gate, up = (dot(mlp_in, lax.all_gather(w, "group", axis=0, tiled=True)) for w in (w_gate, w_up))
    hidden = (jax.nn.silu(gate) * up).astype(BF)
    down_terms = dot(hidden, lax.all_gather(w_down, "group", axis=1, tiled=True))
    mlp_rows = lax.psum_scatter(down_terms.astype(BF), "head", scatter_dimension=0, tiled=True)
    layer_out = (middle.astype(F32) + mlp_rows.astype(F32)).astype(BF)
    return (layer_out, cache_keys, cache_values)


def prepared(x, keep, gain_ref, lhs_ref, coded_ref, squares_ref):
    rows, depth = x.shape
    squares = jnp.broadcast_to(jnp.sum(x * x, axis=1, keepdims=True), (rows, 128))
    scaled = (x * gain_ref[...]).astype(BF)
    if len(lhs_ref.shape) == 2:
        lhs_ref[...] = scaled
    else:
        wide = lhs_ref.shape[2]
        for i in range(lhs_ref.shape[0]):
            lhs_ref[i] = scaled[:, i * wide : (i + 1) * wide]
    high = squares.astype(BF).astype(F32)
    lane = lax.broadcasted_iota(jnp.int32, (rows, 128), 1)
    coded_ref[...] = jnp.where(lane < 64, high, squares - high)[keep:].astype(BF)
    squares_ref[...] = squares[:keep]


def arranged(row, rows_ref, mine_ref, others_ref):
    groups, mine, _ = mine_ref.shape
    for g in range(groups):
        rows_ref[pl.ds(pl.multiple_of(2 * mine * g + row[0] * mine, mine), mine)] = mine_ref[g]
        rows_ref[pl.ds(pl.multiple_of(2 * mine * g + (1 - row[0]) * mine, mine), mine)] = others_ref[g]


def first_kernel(row, mine_ref, others_ref, gain_ref, rows_ref, lhs_ref, coded_ref, squares_ref):
    arranged(row, rows_ref, mine_ref, others_ref)
    prepared(rows_ref[...].astype(F32), squares_ref.shape[0], gain_ref, lhs_ref, coded_ref, squares_ref)


def middle_kernel(row, mine_ref, others_ref, a_ref, b_ref, gain_ref, middle_ref, lhs_ref, coded_ref, squares_ref):
    arranged(row, middle_ref, mine_ref, others_ref)
    total = a_ref[...].astype(F32) + b_ref[...].astype(F32)
    middle_ref[...] = (middle_ref[...].astype(F32) + total).astype(BF)
    prepared(middle_ref[...].astype(F32), squares_ref.shape[0], gain_ref, lhs_ref, coded_ref, squares_ref)


def prepare(kernel, row, operands, rows, depth, keep, cuts, limit=VMEM):
    shapes = [
        jax.ShapeDtypeStruct((rows, depth), BF),
        jax.ShapeDtypeStruct((cuts, rows, depth // cuts) if cuts > 1 else (rows, depth), BF),
        jax.ShapeDtypeStruct((rows - keep, 128), BF),
        jax.ShapeDtypeStruct((keep, 128), F32),
    ]
    def spec(x):
        return pl.BlockSpec(x.shape, lambda j, p: (0,) * len(x.shape))
    return pl.pallas_call(
        kernel,
        grid_spec=pltpu.PrefetchScalarGridSpec(
            num_scalar_prefetch=1,
            grid=(1,),
            in_specs=[spec(x) for x in operands],
            out_specs=[spec(x) for x in shapes],
        ),
        out_shape=shapes,
        compiler_params=pltpu.CompilerParams(vmem_limit_bytes=limit),
    )(row, *operands)


def rows_kernel(place, lhs, coded_ref, *refs):
    weights, (sent_ref, own_ref, held, sems) = refs[:OCT], refs[OCT:]
    block = held.shape[-1]
    keep, width = own_ref.shape
    wide = weights[0].shape[0]
    steps = width // block

    def copies(step):
        for k, w in enumerate(weights):
            at = pl.multiple_of((place[0] ^ k) * wide, wide)
            yield pltpu.make_async_copy(
                w.at[:, step * block : (step + 1) * block], held.at[step % 2, pl.ds(at, wide)], sems.at[step % 2, k]
            )

    for c in copies(0):
        c.start()
    if sent_ref.shape[1] > width:
        sent_ref[:, width:] = coded_ref[...]
    for step in range(steps):
        if step + 1 < steps:
            for c in copies(step + 1):
                c.start()
        for c in copies(step):
            c.wait()
        total = dot(lhs[...], held[step % 2])
        at = step * block
        own_ref[:, at : at + block] = total[:keep]
        sent_ref[:, at : at + block] = total[keep:].astype(BF)


def in_hbm(pieces):
    return [pl.BlockSpec(memory_space=pltpu.HBM)] * len(pieces)


def rows_product(place, lhs, coded, pieces, block, with_squares):
    rows, depth = lhs.shape
    keep = rows // 2
    width = pieces[0].shape[1]
    sent = width + (128 if with_squares else 0)
    whole = lambda j, p: (0, 0)
    return pl.pallas_call(
        rows_kernel,
        grid_spec=pltpu.PrefetchScalarGridSpec(
            num_scalar_prefetch=1,
            grid=(1,),
            in_specs=[pl.BlockSpec(lhs.shape, whole), pl.BlockSpec(coded.shape, whole)] + in_hbm(pieces),
            out_specs=[pl.BlockSpec((keep, sent), whole), pl.BlockSpec((keep, width), whole)],
            scratch_shapes=[pltpu.VMEM((2, depth, block), BF), pltpu.SemaphoreType.DMA((2, OCT))],
        ),
        out_shape=[jax.ShapeDtypeStruct((keep, sent), BF), jax.ShapeDtypeStruct((keep, width), F32)],
        compiler_params=pltpu.CompilerParams(vmem_limit_bytes=VMEM),
    )(place, lhs, coded, *pieces)


def first_rows_kernel(place, lhs, coded_ref, *refs):
    weights, sent_refs, own_ref = refs[:12], refs[12:15], refs[15]
    step = pl.program_id(0)
    block = weights[0].shape[-1]
    keep, width = own_ref.shape

    @pl.when(step == 0)
    def _():
        for g, sent_ref in enumerate(sent_refs):
            sent_ref[:, width:] = coded_ref[g * keep : (g + 1) * keep]

    for i in range(3):
        total = None
        for k in range(4):
            term = dot(lhs[place[0] ^ k], weights[4 * i + k][...])
            total = term if total is None else total + term
        columns = pl.ds(pl.multiple_of(i * (width // 3) + step * block, 128), block)
        own_ref[:, columns] = total[:keep]
        for g, sent_ref in enumerate(sent_refs):
            sent_ref[:, columns] = total[(g + 1) * keep : (g + 2) * keep].astype(BF)


def first_rows_product(place, lhs, coded, pieces, block):
    _, rows, wide = lhs.shape
    keep = rows // 4
    each = pieces[0].shape[1]
    width = 3 * each
    whole = lambda j, p: (0, 0)
    sent = jax.ShapeDtypeStruct((keep, width + 128), BF)
    return pl.pallas_call(
        first_rows_kernel,
        grid_spec=pltpu.PrefetchScalarGridSpec(
            num_scalar_prefetch=1,
            grid=(each // block,),
            in_specs=[pl.BlockSpec(lhs.shape, lambda j, p: (0, 0, 0)), pl.BlockSpec(coded.shape, whole)]
            + [pl.BlockSpec((wide, block), lambda j, p: (0, j))] * len(pieces),
            out_specs=[pl.BlockSpec(sent.shape, whole)] * 3 + [pl.BlockSpec((keep, width), whole)],
        ),
        out_shape=[sent] * 3 + [jax.ShapeDtypeStruct((keep, width), F32)],
        compiler_params=pltpu.CompilerParams(vmem_limit_bytes=VMEM_ALL),
    )(place, lhs, coded, *pieces)


def stacked(a_ref, own_ref, got_ref):
    keep, depth = own_ref.shape
    for h in range(2):
        columns = slice(h * depth // 2, (h + 1) * depth // 2)
        a_ref[2 * h * keep : (2 * h + 1) * keep] = own_ref[:, columns]
        a_ref[(2 * h + 1) * keep : (2 * h + 2) * keep] = got_ref[:, columns]


def columns_kernel(place, own_ref, got_ref, *refs):
    weights, (out_ref, parts, a_ref, held, sems) = refs[:OCT], refs[OCT:]
    keep, depth = own_ref.shape
    wide = held.shape[2] // 2
    copies = [pltpu.make_async_copy(w, held.at[n], sems.at[n]) for n, w in enumerate(weights)]
    for c in copies:
        c.start()
    stacked(a_ref, own_ref, got_ref)
    for k in range(OCT):
        copies[k].wait()
        both = dot(a_ref[...], held[k])
        parts[place[0] ^ k] = (both[: 2 * keep, :wide] + both[2 * keep :, wide:]).astype(BF)
    for i in range(OCT):
        out_ref[:, i * wide : (i + 1) * wide] = parts[i]


def columns_product(place, own, got, pieces):
    keep, depth = own.shape
    rows = 2 * keep
    deep, double = pieces[0].shape
    wide = double // 2
    whole = lambda j, p: (0, 0)
    return pl.pallas_call(
        columns_kernel,
        grid_spec=pltpu.PrefetchScalarGridSpec(
            num_scalar_prefetch=1,
            grid=(1,),
            in_specs=[pl.BlockSpec((keep, depth), whole)] * 2 + in_hbm(pieces),
            out_specs=pl.BlockSpec((rows, OCT * wide), whole),
            scratch_shapes=[
                pltpu.VMEM((OCT, rows, wide), BF),
                pltpu.VMEM((2 * rows, depth // 2), BF),
                pltpu.VMEM((OCT, deep, double), BF),
                pltpu.SemaphoreType.DMA((OCT,)),
            ],
        ),
        out_shape=jax.ShapeDtypeStruct((rows, OCT * wide), BF),
        compiler_params=pltpu.CompilerParams(vmem_limit_bytes=VMEM),
    )(place, own, got, *pieces)


def out_kernel(place, own_ref, got_ref, *refs):
    weights, (out_ref, parts, a_ref) = refs[:OCT], refs[OCT:]
    keep, depth = own_ref.shape
    stacked(a_ref, own_ref, got_ref)
    wide = weights[0].shape[-1] // 2
    for k in range(OCT):
        both = dot(a_ref[...], weights[k][...])
        parts[place[0] ^ k] = (both[: 2 * keep, :wide] + both[2 * keep :, wide:]).astype(BF)
    for i in range(OCT):
        out_ref[:, i * wide : (i + 1) * wide] = parts[i]


def out_product(place, own, got, pieces):
    keep, depth = own.shape
    rows = 2 * keep
    deep, double = pieces[0].shape
    wide = double // 2
    whole = lambda j, p: (0, 0)
    return pl.pallas_call(
        out_kernel,
        grid_spec=pltpu.PrefetchScalarGridSpec(
            num_scalar_prefetch=1,
            grid=(1,),
            in_specs=[pl.BlockSpec((keep, depth), whole)] * 2 + [pl.BlockSpec((deep, double), whole)] * OCT,
            out_specs=pl.BlockSpec((rows, OCT * wide), whole),
            scratch_shapes=[pltpu.VMEM((OCT, rows, wide), BF), pltpu.VMEM((2 * rows, depth // 2), BF)],
        ),
        out_shape=jax.ShapeDtypeStruct((rows, OCT * wide), BF),
        compiler_params=pltpu.CompilerParams(vmem_limit_bytes=VMEM_ALL),
    )(place, own, got, *pieces)


def attention_kernel(model, *refs):
    own, *got = refs[:4]
    squares, cosine, left, right, seg_row, seg_col, slot, out_ref, keys_ref, values_ref = refs[4:]
    count, width = out_ref.shape
    heads_here = width // HEAD_DIM
    total = squares[:, :1]
    for g in got:
        last = g[:, 3 * width :].astype(F32)
        total = total + last[:, :1] + last[:, 64:65]
    scale = lax.rsqrt(total / model + EPS)

    def part(i):
        columns = slice(i * width, (i + 1) * width)
        x = own[:, columns]
        for g in got:
            x = x + g[:, columns].astype(F32)
        return x * scale

    query, key, value = part(0), part(1), part(2)

    def rotated(x):
        ahead = pltpu.roll(x, width - HEAD_DIM // 2, 1)
        behind = pltpu.roll(x, HEAD_DIM // 2, 1)
        return (x * cosine[...] + ahead * left[...] + behind * right[...]).astype(BF)

    q_rot, k_rot, v_b = rotated(query), rotated(key), value.astype(BF)
    spot = lax.broadcasted_iota(jnp.int32, (count, count), 0)
    hot = jnp.where(spot == slot[...], 1.0, 0.0).astype(BF)
    keys_ref[...] = dot(hot, k_rot).astype(BF)
    values_ref[...] = dot(hot, v_b).astype(BF)
    lane = lax.broadcasted_iota(jnp.int32, (count, width), 1)
    within = [(lane >= h * HEAD_DIM) & (lane < (h + 1) * HEAD_DIM) for h in range(heads_here)]
    zero = jnp.zeros((count, width), BF)
    spread_q = jnp.concatenate([jnp.where(w, q_rot, zero) for w in within], axis=0)
    scores = lax.dot_general(spread_q, k_rot, (((1,), (1,)), ((), ())), preferred_element_type=F32)
    scores = (scores * (1.0 / HEAD_DIM**0.5)).reshape(heads_here, count, count)
    other = lax.broadcasted_iota(jnp.int32, (count, count), 1)
    allowed = (seg_col[...] == seg_row[...]) & (other <= spot)
    scores = jnp.where(allowed[None], scores, -1e30)
    expo = jnp.exp(scores - jnp.max(scores, axis=-1, keepdims=True))
    probs = (expo / jnp.sum(expo, axis=-1, keepdims=True)).astype(BF)
    mixed = dot(probs.reshape(heads_here * count, count), v_b)
    total = jnp.zeros((count, width), F32)
    for h in range(heads_here):
        total = total + jnp.where(within[h], mixed[h * count : (h + 1) * count], 0.0)
    out_ref[...] = total.astype(BF)


def attend(model, own, got, squares, tables, segment, slots):
    count, width = own.shape[0], own.shape[1] // 3
    out = jax.ShapeDtypeStruct((count, width), BF)
    return pl.pallas_call(
        functools.partial(attention_kernel, model),
        out_shape=[out, out, out],
        compiler_params=pltpu.CompilerParams(vmem_limit_bytes=VMEM_ALL),
    )(own, *got, squares, *tables, segment.reshape(1, count), segment.reshape(count, 1), slots.reshape(1, count))


def rotation_tables(segment, width):
    half = HEAD_DIM // 2
    lane = jnp.arange(width, dtype=jnp.int32)
    freq = 10000.0 ** (-2.0 * (lane % half).astype(F32) / HEAD_DIM)
    angle = positions(segment).astype(F32)[:, None] * freq[None, :]
    first = ((lane % HEAD_DIM) < half)[None, :]
    sine = jnp.sin(angle)
    return jnp.cos(angle), jnp.where(first, -sine, 0.0), jnp.where(first, 0.0, sine)


def after(x, *others):
    return lax.optimization_barrier((x,) + others)[0]


def octet_plan(n_group):
    def swap(bit):
        pairs = [(g, g ^ bit) for g in range(n_group)]
        return lambda x: lax.ppermute(x, "group", pairs)

    core, near, next_to, across = swap(1), swap(2), swap(4), swap(OCT)

    def other_head(x):
        return lax.ppermute(x, "head", [(0, 1), (1, 0)])

    def beside(w):
        depth = w.shape[0]
        return jnp.concatenate([w[: depth // 2], w[depth // 2 :]], axis=1)

    def all_pieces(own, x, z, diagonal, early=(), late=()):
        return [
            own, core(after(own, *early)), x, core(after(x, *early)), z, core(after(z, *early)),
            diagonal, core(after(diagonal, *late)),
        ]

    def turn(k):
        pairs = [(g, (g + k * QUAD) % n_group) for g in range(n_group)]
        return lambda x: lax.ppermute(x, "group", pairs)

    turns = [turn(k) for k in range(4)]

    def per_device(
        tokens, attn_gain, w_query, w_key, w_value, w_out, mlp_gain, w_gate, w_up, w_down, segment_ids, cache_slot,
    ):
        group = lax.axis_index("group")
        side, fourth = group // OCT, group // QUAD
        place = (group % OCT).astype(jnp.int32).reshape(1)
        place4 = (group % QUAD).astype(jnp.int32).reshape(1)
        row = lax.axis_index("head")
        at_row = row.astype(jnp.int32).reshape(1)
        mine, model = tokens.shape
        half, quarter = model // 2, model // 4
        units = w_gate.shape[1]
        width = w_query.shape[1]
        tables = rotation_tables(segment_ids[0], width)
        gain1 = lax.dynamic_slice(attn_gain, (fourth * quarter,), (quarter,)).reshape(1, quarter)
        gain2 = lax.dynamic_slice(mlp_gain, (side * half,), (half,)).reshape(1, half)

        def columns_of(place, wide):
            return lax.dynamic_slice(tokens, (0, place * wide), (mine, wide))

        cut = [columns_of((fourth + k) % 4, quarter) for k in range(4)]
        given = columns_of(1 - side, half)
        cut = lax.optimization_barrier((*cut, given))
        came = [turns[k](cut[k]) for k in (3, 2, 1)]
        x_q, x_k, x_v = near(w_query), near(w_key), near(w_value)
        o_own, d_own = lax.optimization_barrier((beside(w_out), beside(w_down)))
        x_o = near(o_own)
        both = jnp.stack([cut[0], *came])
        gate, up, z_own, given = lax.optimization_barrier((w_gate, w_up, o_own, cut[4], both))[:4]
        partner = across(given)
        z_o, z_g, z_u = next_to(z_own), next_to(gate), next_to(up)
        mine_too = jnp.stack([columns_of(side, half), partner])
        others_too = other_head(mine_too)
        others = other_head(after(both, x_q, gain1, gain2, *tables, z_g, others_too))
        _, lhs, coded, squares = prepare(
            first_kernel, at_row, (both, others, gain1), 8 * mine, quarter, 2 * mine, QUAD, VMEM_ALL
        )
        x_gate, x_up, x_down = lax.optimization_barrier((w_gate, w_up, d_own, x_q, x_k, x_v, x_o, both))[:3]
        x_g, x_u, x_d = near(x_gate), near(x_up), near(x_down)
        pieces = [p for w, x in ((w_query, x_q), (w_key, x_k), (w_value, x_v)) for p in (w, core(w), x, core(x))]
        *sent, own = first_rows_product(place4, after(lhs, partner), coded, pieces, 384)
        *sent, _ = lax.optimization_barrier((*sent, z_o, z_u))[:4]
        got = [turns[k + 1](sent[k]) for k in range(3)]
        d_o = near(after(z_o, sent[0]))
        got = lax.optimization_barrier((*got, d_o, x_g, x_u, x_d))[:3]
        p_o = all_pieces(o_own, x_o, z_o, d_o, (sent[0],), (sent[0],))
        attended, cache_keys, cache_values = attend(model, own, got, squares, tables, segment_ids[0], cache_slot[0])
        d_g, d_u = near(after(z_g, attended)), near(after(z_u, attended))
        got = across(attended)
        z_d = next_to(after(d_own, got))
        terms = out_product(place, attended, got, p_o)
        others = other_head(terms)
        p_g = all_pieces(w_gate, x_g, z_g, d_g, (attended,), (others,))
        middle, lhs, coded, squares = prepare(
            middle_kernel, at_row, (mine_too, others_too, terms, after(others, z_d, d_g), gain2), 4 * mine, half, 2 * mine, 1
        )
        sent_g, own_g = rows_product(place, lhs, coded, p_g, 512, True)
        got_g = across(sent_g)
        p_u = all_pieces(w_up, x_u, z_u, d_u, (lhs,), (got_g,))
        sent_u, own_u = rows_product(place, after(lhs, sent_g), coded, p_u, 512, False)
        got_u = across(sent_u)
        d_d = near(after(z_d, sent_g))
        p_d = all_pieces(d_own, x_d, z_d, d_d, (sent_u,), (got_u,))
        last = got_g[:, units:].astype(F32)
        scale = lax.rsqrt((squares[:, :1] + last[:, :1] + last[:, 64:65]) / model + EPS)
        gate = (own_g + got_g[:, :units].astype(F32)) * scale
        up = (own_u + got_u.astype(F32)) * scale
        hidden = (jax.nn.silu(gate) * up).astype(BF)
        terms = columns_product(place, hidden, across(hidden), p_d).reshape(2, 2, mine, half)
        given = other_head(lax.dynamic_index_in_dim(terms, 1 - row, 1, keepdims=False))
        mlp = lax.dynamic_index_in_dim(terms, row, 1, keepdims=False).astype(F32) + given.astype(F32)
        kept = lax.dynamic_index_in_dim(middle.reshape(2, 2, mine, half), row, 1, keepdims=False)
        out = (kept.astype(F32) + mlp).astype(BF)
        got = across(out[1])
        layer_out = jnp.where(
            side == 0, jnp.concatenate([out[0], got], axis=1), jnp.concatenate([got, out[0]], axis=1)
        )
        return (layer_out, cache_keys, cache_values)

    return per_device


def solution(mesh):
    n_group = mesh.shape["group"]
    in_specs = (
        P(("group", "head"), None),
        P(),
        P("group", "head"),
        P("group", "head"),
        P("group", "head"),
        P("head", "group"),
        P(),
        P("group", "head"),
        P("group", "head"),
        P("head", "group"),
        P("group", None),
        P("group", None),
    )
    out_specs = (P(("group", "head"), None), P("group", "head"), P("group", "head"))
    body = octet_plan(n_group) if n_group == 2 * OCT else gathered_plan
    return jax.shard_map(body, mesh=mesh, in_specs=in_specs, out_specs=out_specs, check_vma=False)
```

```python
import functools

import jax
import jax.numpy as jnp
from jax import lax
from jax.experimental import pallas as pl
from jax.experimental.pallas import tpu as pltpu
from jax.sharding import PartitionSpec as P

HEAD_DIM = 96
EPS = 1e-05
OCT = 8
QUAD = 4
BF = jnp.bfloat16
F32 = jnp.float32
VMEM = 24 * 1024 * 1024
VMEM_ALL = 60 * 1024 * 1024


def norm_rows(rows, gain):
    values = rows.astype(F32)
    scale = lax.rsqrt(jnp.mean(values * values, axis=-1, keepdims=True) + EPS)
    return (values * scale * gain).astype(BF)


def positions(segment):
    count = segment.shape[0]
    index = jnp.arange(count, dtype=jnp.int32)
    before = jnp.concatenate([jnp.full((1,), -1, jnp.int32), segment[:-1]])
    starts = jnp.where(segment != before, index, jnp.zeros_like(index))
    return index - lax.cummax(starts, axis=0)


def rotate(heads, place):
    half = heads.shape[-1] // 2
    freq = 10000.0 ** (-2.0 * jnp.arange(half, dtype=F32) / heads.shape[-1])
    angle = place.astype(F32)[:, None] * freq[None, :]
    cosine = jnp.cos(angle)[:, None, :]
    sine = jnp.sin(angle)[:, None, :]
    first = heads[..., :half]
    second = heads[..., half:]
    return jnp.concatenate(
        [first * cosine - second * sine, second * cosine + first * sine], axis=-1
    )


def dot(a, b):
    return jnp.dot(a, b, preferred_element_type=F32)


def attention(query, key, v_b, segment, slots):
    count, width = v_b.shape
    heads_here = width // HEAD_DIM
    index = jnp.arange(count, dtype=jnp.int32)
    place = positions(segment)
    q_rot = rotate(query.reshape(count, heads_here, HEAD_DIM), place).astype(BF)
    k_rot = rotate(key.reshape(count, heads_here, HEAD_DIM), place).astype(BF)
    k_flat = k_rot.reshape(count, width)
    cache_keys = jnp.zeros_like(k_flat).at[slots].set(k_flat)
    cache_values = jnp.zeros_like(v_b).at[slots].set(v_b)
    allowed = (segment[:, None] == segment[None, :]) & (index[None, :] <= index[:, None])
    scores = jnp.einsum("qhd,khd->hqk", q_rot, k_rot, preferred_element_type=F32)
    scores = scores * (1.0 / HEAD_DIM**0.5)
    scores = jnp.where(allowed[None, :, :], scores, -1e30)
    top = jnp.max(scores, axis=-1, keepdims=True)
    expo = jnp.exp(scores - top)
    probs = (expo / jnp.sum(expo, axis=-1, keepdims=True)).astype(BF)
    v_heads = v_b.reshape(count, heads_here, HEAD_DIM)
    attended = jnp.einsum("hqk,khd->qhd", probs, v_heads, preferred_element_type=F32)
    return attended.astype(BF).reshape(count, width), cache_keys, cache_values


def gathered_plan(
    tokens, attn_gain, w_query, w_key, w_value, w_out, mlp_gain, w_gate, w_up, w_down, segment_ids, cache_slot,
):
    whole = lax.all_gather(norm_rows(tokens, attn_gain), "head", axis=0, tiled=True)
    query, key, value = (
        dot(whole, lax.all_gather(w, "group", axis=0, tiled=True)) for w in (w_query, w_key, w_value)
    )
    attended, cache_keys, cache_values = attention(
        query, key, value.astype(BF), segment_ids[0], cache_slot[0]
    )
    out_terms = dot(attended, lax.all_gather(w_out, "group", axis=1, tiled=True))
    attn_rows = lax.psum_scatter(out_terms.astype(BF), "head", scatter_dimension=0, tiled=True)
    middle = (tokens.astype(F32) + attn_rows.astype(F32)).astype(BF)
    mlp_in = lax.all_gather(norm_rows(middle, mlp_gain), "head", axis=0, tiled=True)
    gate, up = (dot(mlp_in, lax.all_gather(w, "group", axis=0, tiled=True)) for w in (w_gate, w_up))
    hidden = (jax.nn.silu(gate) * up).astype(BF)
    down_terms = dot(hidden, lax.all_gather(w_down, "group", axis=1, tiled=True))
    mlp_rows = lax.psum_scatter(down_terms.astype(BF), "head", scatter_dimension=0, tiled=True)
    layer_out = (middle.astype(F32) + mlp_rows.astype(F32)).astype(BF)
    return (layer_out, cache_keys, cache_values)


def prepared(x, keep, gain_ref, lhs_ref, coded_ref, squares_ref):
    rows, depth = x.shape
    squares = jnp.broadcast_to(jnp.sum(x * x, axis=1, keepdims=True), (rows, 128))
    scaled = (x * gain_ref[...]).astype(BF)
    if len(lhs_ref.shape) == 2:
        lhs_ref[...] = scaled
    else:
        wide = lhs_ref.shape[2]
        for i in range(lhs_ref.shape[0]):
            lhs_ref[i] = scaled[:, i * wide : (i + 1) * wide]
    high = squares.astype(BF).astype(F32)
    lane = lax.broadcasted_iota(jnp.int32, (rows, 128), 1)
    coded_ref[...] = jnp.where(lane < 64, high, squares - high)[keep:].astype(BF)
    squares_ref[...] = squares[:keep]


def arranged(row, rows_ref, mine_ref, others_ref):
    groups, mine, _ = mine_ref.shape
    for g in range(groups):
        rows_ref[pl.ds(pl.multiple_of(2 * mine * g + row[0] * mine, mine), mine)] = mine_ref[g]
        rows_ref[pl.ds(pl.multiple_of(2 * mine * g + (1 - row[0]) * mine, mine), mine)] = others_ref[g]


def first_kernel(row, mine_ref, others_ref, gain_ref, rows_ref, lhs_ref, coded_ref, squares_ref):
    arranged(row, rows_ref, mine_ref, others_ref)
    prepared(rows_ref[...].astype(F32), squares_ref.shape[0], gain_ref, lhs_ref, coded_ref, squares_ref)


def middle_kernel(row, mine_ref, others_ref, a_ref, b_ref, gain_ref, middle_ref, lhs_ref, coded_ref, squares_ref):
    arranged(row, middle_ref, mine_ref, others_ref)
    total = a_ref[...].astype(F32) + b_ref[...].astype(F32)
    middle_ref[...] = (middle_ref[...].astype(F32) + total).astype(BF)
    prepared(middle_ref[...].astype(F32), squares_ref.shape[0], gain_ref, lhs_ref, coded_ref, squares_ref)


def prepare(kernel, row, operands, rows, depth, keep, cuts, limit=VMEM):
    shapes = [
        jax.ShapeDtypeStruct((rows, depth), BF),
        jax.ShapeDtypeStruct((cuts, rows, depth // cuts) if cuts > 1 else (rows, depth), BF),
        jax.ShapeDtypeStruct((rows - keep, 128), BF),
        jax.ShapeDtypeStruct((keep, 128), F32),
    ]
    def spec(x):
        return pl.BlockSpec(x.shape, lambda j, p: (0,) * len(x.shape))
    return pl.pallas_call(
        kernel,
        grid_spec=pltpu.PrefetchScalarGridSpec(
            num_scalar_prefetch=1,
            grid=(1,),
            in_specs=[spec(x) for x in operands],
            out_specs=[spec(x) for x in shapes],
        ),
        out_shape=shapes,
        compiler_params=pltpu.CompilerParams(vmem_limit_bytes=limit),
    )(row, *operands)


def rows_kernel(place, lhs, coded_ref, *refs):
    weights, (sent_ref, own_ref, held, sems) = refs[:OCT], refs[OCT:]
    block = held.shape[-1]
    keep, width = own_ref.shape
    wide = weights[0].shape[0]
    steps = width // block

    def copies(step):
        for k, w in enumerate(weights):
            at = pl.multiple_of((place[0] ^ k) * wide, wide)
            yield pltpu.make_async_copy(
                w.at[:, step * block : (step + 1) * block], held.at[step, pl.ds(at, wide)], sems.at[step, k]
            )

    for step in range(steps):
        for c in copies(step):
            c.start()
    if sent_ref.shape[1] > width:
        sent_ref[:, width:] = coded_ref[...]
    for step in range(steps):
        for c in copies(step):
            c.wait()
        total = dot(lhs[...], held[step])
        at = step * block
        own_ref[:, at : at + block] = total[:keep]
        sent_ref[:, at : at + block] = total[keep:].astype(BF)


def in_hbm(pieces):
    return [pl.BlockSpec(memory_space=pltpu.HBM)] * len(pieces)


def rows_product(place, lhs, coded, pieces, block, with_squares):
    rows, depth = lhs.shape
    keep = rows // 2
    width = pieces[0].shape[1]
    sent = width + (128 if with_squares else 0)
    whole = lambda j, p: (0, 0)
    return pl.pallas_call(
        rows_kernel,
        grid_spec=pltpu.PrefetchScalarGridSpec(
            num_scalar_prefetch=1,
            grid=(1,),
            in_specs=[pl.BlockSpec(lhs.shape, whole), pl.BlockSpec(coded.shape, whole)] + in_hbm(pieces),
            out_specs=[pl.BlockSpec((keep, sent), whole), pl.BlockSpec((keep, width), whole)],
            scratch_shapes=[pltpu.VMEM((width // block, depth, block), BF), pltpu.SemaphoreType.DMA((width // block, OCT))],
        ),
        out_shape=[jax.ShapeDtypeStruct((keep, sent), BF), jax.ShapeDtypeStruct((keep, width), F32)],
        compiler_params=pltpu.CompilerParams(vmem_limit_bytes=VMEM),
    )(place, lhs, coded, *pieces)


def first_rows_kernel(place, lhs, coded_ref, *refs):
    weights, sent_refs, own_ref = refs[:12], refs[12:15], refs[15]
    step = pl.program_id(0)
    block = weights[0].shape[-1]
    keep, width = own_ref.shape

    @pl.when(step == 0)
    def _():
        for g, sent_ref in enumerate(sent_refs):
            sent_ref[:, width:] = coded_ref[g * keep : (g + 1) * keep]

    for i in range(3):
        total = None
        for k in range(4):
            term = dot(lhs[place[0] ^ k], weights[4 * i + k][...])
            total = term if total is None else total + term
        columns = pl.ds(pl.multiple_of(i * (width // 3) + step * block, 128), block)
        own_ref[:, columns] = total[:keep]
        for g, sent_ref in enumerate(sent_refs):
            sent_ref[:, columns] = total[(g + 1) * keep : (g + 2) * keep].astype(BF)


def first_rows_product(place, lhs, coded, pieces, block):
    _, rows, wide = lhs.shape
    keep = rows // 4
    each = pieces[0].shape[1]
    width = 3 * each
    whole = lambda j, p: (0, 0)
    sent = jax.ShapeDtypeStruct((keep, width + 128), BF)
    return pl.pallas_call(
        first_rows_kernel,
        grid_spec=pltpu.PrefetchScalarGridSpec(
            num_scalar_prefetch=1,
            grid=(each // block,),
            in_specs=[pl.BlockSpec(lhs.shape, lambda j, p: (0, 0, 0)), pl.BlockSpec(coded.shape, whole)]
            + [pl.BlockSpec((wide, block), lambda j, p: (0, j))] * len(pieces),
            out_specs=[pl.BlockSpec(sent.shape, whole)] * 3 + [pl.BlockSpec((keep, width), whole)],
        ),
        out_shape=[sent] * 3 + [jax.ShapeDtypeStruct((keep, width), F32)],
        compiler_params=pltpu.CompilerParams(vmem_limit_bytes=VMEM_ALL),
    )(place, lhs, coded, *pieces)


def columns_kernel(place, own_ref, got_ref, *refs):
    weights, (out_ref, parts, a_ref, held, sems) = refs[:OCT], refs[OCT:]
    keep, depth = own_ref.shape
    wide = held.shape[2] // 2
    copies = [pltpu.make_async_copy(w, held.at[n], sems.at[n]) for n, w in enumerate(weights)]
    for c in copies:
        c.start()
    a_ref[:keep] = own_ref[...]
    a_ref[keep:] = got_ref[...]
    for k in range(OCT):
        copies[k].wait()
        lower = dot(a_ref[:, : depth // 2], held[k])
        upper = dot(a_ref[:, depth // 2 :], held[k])
        parts[place[0] ^ k] = (lower[:, :wide] + upper[:, wide:]).astype(BF)
    for i in range(OCT):
        out_ref[:, i * wide : (i + 1) * wide] = parts[i]


def columns_product(place, own, got, pieces):
    keep, depth = own.shape
    rows = 2 * keep
    deep, double = pieces[0].shape
    wide = double // 2
    whole = lambda j, p: (0, 0)
    return pl.pallas_call(
        columns_kernel,
        grid_spec=pltpu.PrefetchScalarGridSpec(
            num_scalar_prefetch=1,
            grid=(1,),
            in_specs=[pl.BlockSpec((keep, depth), whole)] * 2 + in_hbm(pieces),
            out_specs=pl.BlockSpec((rows, OCT * wide), whole),
            scratch_shapes=[
                pltpu.VMEM((OCT, rows, wide), BF),
                pltpu.VMEM((rows, depth), BF),
                pltpu.VMEM((OCT, deep, double), BF),
                pltpu.SemaphoreType.DMA((OCT,)),
            ],
        ),
        out_shape=jax.ShapeDtypeStruct((rows, OCT * wide), BF),
        compiler_params=pltpu.CompilerParams(vmem_limit_bytes=VMEM),
    )(place, own, got, *pieces)


def out_kernel(place, own_ref, got_ref, *refs):
    weights, (out_ref, parts, a_ref) = refs[:OCT], refs[OCT:]
    keep, depth = own_ref.shape
    a_ref[:keep] = own_ref[...]
    a_ref[keep:] = got_ref[...]
    wide = weights[0].shape[-1] // 2
    for k in range(OCT):
        lower = dot(a_ref[:, : depth // 2], weights[k][...])
        upper = dot(a_ref[:, depth // 2 :], weights[k][...])
        parts[place[0] ^ k] = (lower[:, :wide] + upper[:, wide:]).astype(BF)
    for i in range(OCT):
        out_ref[:, i * wide : (i + 1) * wide] = parts[i]


def out_product(place, own, got, pieces):
    keep, depth = own.shape
    rows = 2 * keep
    deep, double = pieces[0].shape
    wide = double // 2
    whole = lambda j, p: (0, 0)
    return pl.pallas_call(
        out_kernel,
        grid_spec=pltpu.PrefetchScalarGridSpec(
            num_scalar_prefetch=1,
            grid=(1,),
            in_specs=[pl.BlockSpec((keep, depth), whole)] * 2 + [pl.BlockSpec((deep, double), whole)] * OCT,
            out_specs=pl.BlockSpec((rows, OCT * wide), whole),
            scratch_shapes=[pltpu.VMEM((OCT, rows, wide), BF), pltpu.VMEM((rows, depth), BF)],
        ),
        out_shape=jax.ShapeDtypeStruct((rows, OCT * wide), BF),
        compiler_params=pltpu.CompilerParams(vmem_limit_bytes=VMEM_ALL),
    )(place, own, got, *pieces)


def attention_kernel(model, *refs):
    own, *got = refs[:4]
    squares, cosine, left, right, seg_row, seg_col, slot, out_ref, keys_ref, values_ref = refs[4:]
    count, width = out_ref.shape
    heads_here = width // HEAD_DIM
    total = squares[:, :1]
    for g in got:
        last = g[:, 3 * width :].astype(F32)
        total = total + last[:, :1] + last[:, 64:65]
    scale = lax.rsqrt(total / model + EPS)

    def part(i):
        columns = slice(i * width, (i + 1) * width)
        x = own[:, columns]
        for g in got:
            x = x + g[:, columns].astype(F32)
        return x * scale

    query, key, value = part(0), part(1), part(2)

    def rotated(x):
        ahead = pltpu.roll(x, width - HEAD_DIM // 2, 1)
        behind = pltpu.roll(x, HEAD_DIM // 2, 1)
        return (x * cosine[...] + ahead * left[...] + behind * right[...]).astype(BF)

    q_rot, k_rot, v_b = rotated(query), rotated(key), value.astype(BF)
    spot = lax.broadcasted_iota(jnp.int32, (count, count), 0)
    hot = jnp.where(spot == slot[...], 1.0, 0.0).astype(BF)
    keys_ref[...] = dot(hot, k_rot).astype(BF)
    values_ref[...] = dot(hot, v_b).astype(BF)
    lane = lax.broadcasted_iota(jnp.int32, (count, width), 1)
    within = [(lane >= h * HEAD_DIM) & (lane < (h + 1) * HEAD_DIM) for h in range(heads_here)]
    zero = jnp.zeros((count, width), BF)
    spread_q = jnp.concatenate([jnp.where(w, q_rot, zero) for w in within], axis=0)
    scores = lax.dot_general(spread_q, k_rot, (((1,), (1,)), ((), ())), preferred_element_type=F32)
    scores = (scores * (1.0 / HEAD_DIM**0.5)).reshape(heads_here, count, count)
    other = lax.broadcasted_iota(jnp.int32, (count, count), 1)
    allowed = (seg_col[...] == seg_row[...]) & (other <= spot)
    scores = jnp.where(allowed[None], scores, -1e30)
    expo = jnp.exp(scores - jnp.max(scores, axis=-1, keepdims=True))
    probs = (expo / jnp.sum(expo, axis=-1, keepdims=True)).astype(BF)
    mixed = dot(probs.reshape(heads_here * count, count), v_b)
    total = jnp.zeros((count, width), F32)
    for h in range(heads_here):
        total = total + jnp.where(within[h], mixed[h * count : (h + 1) * count], 0.0)
    out_ref[...] = total.astype(BF)


def attend(model, own, got, squares, tables, segment, slots):
    count, width = own.shape[0], own.shape[1] // 3
    out = jax.ShapeDtypeStruct((count, width), BF)
    return pl.pallas_call(
        functools.partial(attention_kernel, model),
        out_shape=[out, out, out],
        compiler_params=pltpu.CompilerParams(vmem_limit_bytes=VMEM_ALL),
    )(own, *got, squares, *tables, segment.reshape(1, count), segment.reshape(count, 1), slots.reshape(1, count))


def rotation_tables(segment, width):
    half = HEAD_DIM // 2
    lane = jnp.arange(width, dtype=jnp.int32)
    freq = 10000.0 ** (-2.0 * (lane % half).astype(F32) / HEAD_DIM)
    angle = positions(segment).astype(F32)[:, None] * freq[None, :]
    first = ((lane % HEAD_DIM) < half)[None, :]
    sine = jnp.sin(angle)
    return jnp.cos(angle), jnp.where(first, -sine, 0.0), jnp.where(first, 0.0, sine)


def after(x, *others):
    return lax.optimization_barrier((x,) + others)[0]


def octet_plan(n_group):
    def swap(bit):
        pairs = [(g, g ^ bit) for g in range(n_group)]
        return lambda x: lax.ppermute(x, "group", pairs)

    core, near, next_to, across = swap(1), swap(2), swap(4), swap(OCT)

    def other_head(x):
        return lax.ppermute(x, "head", [(0, 1), (1, 0)])

    def beside(w):
        depth = w.shape[0]
        return jnp.concatenate([w[: depth // 2], w[depth // 2 :]], axis=1)

    def all_pieces(own, x, z, diagonal, early=(), late=()):
        return [
            own, core(after(own, *early)), x, core(after(x, *early)), z, core(after(z, *early)),
            diagonal, core(after(diagonal, *late)),
        ]

    def turn(k):
        pairs = [(g, (g + k * QUAD) % n_group) for g in range(n_group)]
        return lambda x: lax.ppermute(x, "group", pairs)

    turns = [turn(k) for k in range(4)]

    def per_device(
        tokens, attn_gain, w_query, w_key, w_value, w_out, mlp_gain, w_gate, w_up, w_down, segment_ids, cache_slot,
    ):
        group = lax.axis_index("group")
        side, fourth = group // OCT, group // QUAD
        place = (group % OCT).astype(jnp.int32).reshape(1)
        place4 = (group % QUAD).astype(jnp.int32).reshape(1)
        row = lax.axis_index("head")
        at_row = row.astype(jnp.int32).reshape(1)
        mine, model = tokens.shape
        half, quarter = model // 2, model // 4
        units = w_gate.shape[1]
        width = w_query.shape[1]
        tables = rotation_tables(segment_ids[0], width)
        gain1 = lax.dynamic_slice(attn_gain, (fourth * quarter,), (quarter,)).reshape(1, quarter)
        gain2 = lax.dynamic_slice(mlp_gain, (side * half,), (half,)).reshape(1, half)

        def columns_of(place, wide):
            return lax.dynamic_slice(tokens, (0, place * wide), (mine, wide))

        cut = [columns_of((fourth + k) % 4, quarter) for k in range(4)]
        given = columns_of(1 - side, half)
        cut = lax.optimization_barrier((*cut, given))
        came = [turns[k](cut[k]) for k in (3, 2, 1)]
        x_q, x_k, x_v = near(w_query), near(w_key), near(w_value)
        o_own, d_own = lax.optimization_barrier((beside(w_out), beside(w_down)))
        x_o = near(o_own)
        both = jnp.stack([cut[0], *came])
        partner = across(after(cut[4], both))
        gate, up, z_own = lax.optimization_barrier((w_gate, w_up, o_own, both, partner))[:3]
        z_o, z_g, z_u = next_to(z_own), next_to(gate), next_to(up)
        mine_too = jnp.stack([columns_of(side, half), partner])
        others_too = other_head(mine_too)
        others = other_head(after(both, x_q, gain1, gain2, *tables, z_g, others_too))
        _, lhs, coded, squares = prepare(
            first_kernel, at_row, (both, others, gain1), 8 * mine, quarter, 2 * mine, QUAD, VMEM_ALL
        )
        x_gate, x_up, x_down = lax.optimization_barrier((w_gate, w_up, d_own, x_q, x_k, x_v, x_o, both))[:3]
        x_g, x_u, x_d = near(x_gate), near(x_up), near(x_down)
        pieces = [p for w, x in ((w_query, x_q), (w_key, x_k), (w_value, x_v)) for p in (w, core(w), x, core(x))]
        *sent, own = first_rows_product(place4, after(lhs, partner), coded, pieces, 384)
        *sent, _ = lax.optimization_barrier((*sent, z_o, z_u))[:4]
        got = [turns[k + 1](sent[k]) for k in range(3)]
        d_o = near(after(z_o, sent[0]))
        got = lax.optimization_barrier((*got, d_o, x_g, x_u, x_d))[:3]
        p_o = all_pieces(o_own, x_o, z_o, d_o, (sent[0],), (sent[0],))
        attended, cache_keys, cache_values = attend(model, own, got, squares, tables, segment_ids[0], cache_slot[0])
        d_g, d_u = near(after(z_g, attended)), near(after(z_u, attended))
        got = across(attended)
        z_d = next_to(after(d_own, got))
        terms = out_product(place, attended, got, p_o)
        others = other_head(terms)
        p_g = all_pieces(w_gate, x_g, z_g, d_g, (attended,), (others,))
        middle, lhs, coded, squares = prepare(
            middle_kernel, at_row, (mine_too, others_too, terms, after(others, z_d, d_g), gain2), 4 * mine, half, 2 * mine, 1
        )
        sent_g, own_g = rows_product(place, lhs, coded, p_g, 512, True)
        got_g = across(sent_g)
        p_u = all_pieces(w_up, x_u, z_u, d_u, (lhs,), (got_g,))
        sent_u, own_u = rows_product(place, after(lhs, sent_g), coded, p_u, 512, False)
        got_u = across(sent_u)
        d_d = near(after(z_d, sent_g))
        p_d = all_pieces(d_own, x_d, z_d, d_d, (sent_u,), (got_u,))
        last = got_g[:, units:].astype(F32)
        scale = lax.rsqrt((squares[:, :1] + last[:, :1] + last[:, 64:65]) / model + EPS)
        gate = (own_g + got_g[:, :units].astype(F32)) * scale
        up = (own_u + got_u.astype(F32)) * scale
        hidden = (jax.nn.silu(gate) * up).astype(BF)
        terms = columns_product(place, hidden, across(hidden), p_d).reshape(2, 2, mine, half)
        given = other_head(lax.dynamic_index_in_dim(terms, 1 - row, 1, keepdims=False))
        mlp = lax.dynamic_index_in_dim(terms, row, 1, keepdims=False).astype(F32) + given.astype(F32)
        kept = lax.dynamic_index_in_dim(middle.reshape(2, 2, mine, half), row, 1, keepdims=False)
        out = (kept.astype(F32) + mlp).astype(BF)
        got = across(out[1])
        layer_out = jnp.where(
            side == 0, jnp.concatenate([out[0], got], axis=1), jnp.concatenate([got, out[0]], axis=1)
        )
        return (layer_out, cache_keys, cache_values)

    return per_device


def solution(mesh):
    n_group = mesh.shape["group"]
    in_specs = (
        P(("group", "head"), None),
        P(),
        P("group", "head"),
        P("group", "head"),
        P("group", "head"),
        P("head", "group"),
        P(),
        P("group", "head"),
        P("group", "head"),
        P("head", "group"),
        P("group", None),
        P("group", None),
    )
    out_specs = (P(("group", "head"), None), P("group", "head"), P("group", "head"))
    body = octet_plan(n_group) if n_group == 2 * OCT else gathered_plan
    return jax.shard_map(body, mesh=mesh, in_specs=in_specs, out_specs=out_specs, check_vma=False)
```

```python
import functools

import jax
import jax.numpy as jnp
from jax import lax
from jax.experimental import pallas as pl
from jax.experimental.pallas import tpu as pltpu
from jax.sharding import PartitionSpec as P

HEAD_DIM = 96
EPS = 1e-05
OCT = 8
QUAD = 4
BF = jnp.bfloat16
F32 = jnp.float32
VMEM = 24 * 1024 * 1024
VMEM_ALL = 60 * 1024 * 1024


def norm_rows(rows, gain):
    values = rows.astype(F32)
    scale = lax.rsqrt(jnp.mean(values * values, axis=-1, keepdims=True) + EPS)
    return (values * scale * gain).astype(BF)


def positions(segment):
    count = segment.shape[0]
    index = jnp.arange(count, dtype=jnp.int32)
    before = jnp.concatenate([jnp.full((1,), -1, jnp.int32), segment[:-1]])
    starts = jnp.where(segment != before, index, jnp.zeros_like(index))
    return index - lax.cummax(starts, axis=0)


def rotate(heads, place):
    half = heads.shape[-1] // 2
    freq = 10000.0 ** (-2.0 * jnp.arange(half, dtype=F32) / heads.shape[-1])
    angle = place.astype(F32)[:, None] * freq[None, :]
    cosine = jnp.cos(angle)[:, None, :]
    sine = jnp.sin(angle)[:, None, :]
    first = heads[..., :half]
    second = heads[..., half:]
    return jnp.concatenate(
        [first * cosine - second * sine, second * cosine + first * sine], axis=-1
    )


def dot(a, b):
    return jnp.dot(a, b, preferred_element_type=F32)


def attention(query, key, v_b, segment, slots):
    count, width = v_b.shape
    heads_here = width // HEAD_DIM
    index = jnp.arange(count, dtype=jnp.int32)
    place = positions(segment)
    q_rot = rotate(query.reshape(count, heads_here, HEAD_DIM), place).astype(BF)
    k_rot = rotate(key.reshape(count, heads_here, HEAD_DIM), place).astype(BF)
    k_flat = k_rot.reshape(count, width)
    cache_keys = jnp.zeros_like(k_flat).at[slots].set(k_flat)
    cache_values = jnp.zeros_like(v_b).at[slots].set(v_b)
    allowed = (segment[:, None] == segment[None, :]) & (index[None, :] <= index[:, None])
    scores = jnp.einsum("qhd,khd->hqk", q_rot, k_rot, preferred_element_type=F32)
    scores = scores * (1.0 / HEAD_DIM**0.5)
    scores = jnp.where(allowed[None, :, :], scores, -1e30)
    top = jnp.max(scores, axis=-1, keepdims=True)
    expo = jnp.exp(scores - top)
    probs = (expo / jnp.sum(expo, axis=-1, keepdims=True)).astype(BF)
    v_heads = v_b.reshape(count, heads_here, HEAD_DIM)
    attended = jnp.einsum("hqk,khd->qhd", probs, v_heads, preferred_element_type=F32)
    return attended.astype(BF).reshape(count, width), cache_keys, cache_values


def gathered_plan(
    tokens, attn_gain, w_query, w_key, w_value, w_out, mlp_gain, w_gate, w_up, w_down, segment_ids, cache_slot,
):
    whole = lax.all_gather(norm_rows(tokens, attn_gain), "head", axis=0, tiled=True)
    query, key, value = (
        dot(whole, lax.all_gather(w, "group", axis=0, tiled=True)) for w in (w_query, w_key, w_value)
    )
    attended, cache_keys, cache_values = attention(
        query, key, value.astype(BF), segment_ids[0], cache_slot[0]
    )
    out_terms = dot(attended, lax.all_gather(w_out, "group", axis=1, tiled=True))
    attn_rows = lax.psum_scatter(out_terms.astype(BF), "head", scatter_dimension=0, tiled=True)
    middle = (tokens.astype(F32) + attn_rows.astype(F32)).astype(BF)
    mlp_in = lax.all_gather(norm_rows(middle, mlp_gain), "head", axis=0, tiled=True)
    gate, up = (dot(mlp_in, lax.all_gather(w, "group", axis=0, tiled=True)) for w in (w_gate, w_up))
    hidden = (jax.nn.silu(gate) * up).astype(BF)
    down_terms = dot(hidden, lax.all_gather(w_down, "group", axis=1, tiled=True))
    mlp_rows = lax.psum_scatter(down_terms.astype(BF), "head", scatter_dimension=0, tiled=True)
    layer_out = (middle.astype(F32) + mlp_rows.astype(F32)).astype(BF)
    return (layer_out, cache_keys, cache_values)


def prepared(x, keep, gain_ref, lhs_ref, coded_ref, squares_ref):
    rows, depth = x.shape
    squares = jnp.broadcast_to(jnp.sum(x * x, axis=1, keepdims=True), (rows, 128))
    scaled = (x * gain_ref[...]).astype(BF)
    if len(lhs_ref.shape) == 2:
        lhs_ref[...] = scaled
    else:
        wide = lhs_ref.shape[2]
        for i in range(lhs_ref.shape[0]):
            lhs_ref[i] = scaled[:, i * wide : (i + 1) * wide]
    high = squares.astype(BF).astype(F32)
    lane = lax.broadcasted_iota(jnp.int32, (rows, 128), 1)
    coded_ref[...] = jnp.where(lane < 64, high, squares - high)[keep:].astype(BF)
    squares_ref[...] = squares[:keep]


def arranged(row, rows_ref, mine_ref, others_ref):
    groups, mine, _ = mine_ref.shape
    for g in range(groups):
        rows_ref[pl.ds(pl.multiple_of(2 * mine * g + row[0] * mine, mine), mine)] = mine_ref[g]
        rows_ref[pl.ds(pl.multiple_of(2 * mine * g + (1 - row[0]) * mine, mine), mine)] = others_ref[g]


def first_kernel(row, mine_ref, others_ref, gain_ref, rows_ref, lhs_ref, coded_ref, squares_ref):
    arranged(row, rows_ref, mine_ref, others_ref)
    prepared(rows_ref[...].astype(F32), squares_ref.shape[0], gain_ref, lhs_ref, coded_ref, squares_ref)


def middle_kernel(row, mine_ref, others_ref, a_ref, b_ref, gain_ref, middle_ref, lhs_ref, coded_ref, squares_ref):
    arranged(row, middle_ref, mine_ref, others_ref)
    total = a_ref[...].astype(F32) + b_ref[...].astype(F32)
    middle_ref[...] = (middle_ref[...].astype(F32) + total).astype(BF)
    prepared(middle_ref[...].astype(F32), squares_ref.shape[0], gain_ref, lhs_ref, coded_ref, squares_ref)


def prepare(kernel, row, operands, rows, depth, keep, cuts, limit=VMEM):
    shapes = [
        jax.ShapeDtypeStruct((rows, depth), BF),
        jax.ShapeDtypeStruct((cuts, rows, depth // cuts) if cuts > 1 else (rows, depth), BF),
        jax.ShapeDtypeStruct((rows - keep, 128), BF),
        jax.ShapeDtypeStruct((keep, 128), F32),
    ]
    def spec(x):
        return pl.BlockSpec(x.shape, lambda j, p: (0,) * len(x.shape))
    return pl.pallas_call(
        kernel,
        grid_spec=pltpu.PrefetchScalarGridSpec(
            num_scalar_prefetch=1,
            grid=(1,),
            in_specs=[spec(x) for x in operands],
            out_specs=[spec(x) for x in shapes],
        ),
        out_shape=shapes,
        compiler_params=pltpu.CompilerParams(vmem_limit_bytes=limit),
    )(row, *operands)


def rows_kernel(place, lhs, coded_ref, *refs):
    weights, (sent_ref, own_ref, held, sems) = refs[:OCT], refs[OCT:]
    block = held.shape[-1]
    keep, width = own_ref.shape
    wide = weights[0].shape[0]
    steps = width // block

    def copies(step):
        for k, w in enumerate(weights):
            at = pl.multiple_of((place[0] ^ k) * wide, wide)
            yield pltpu.make_async_copy(
                w.at[:, step * block : (step + 1) * block], held.at[step, pl.ds(at, wide)], sems.at[step, k]
            )

    for step in range(steps):
        for c in copies(step):
            c.start()
    if sent_ref.shape[1] > width:
        sent_ref[:, width:] = coded_ref[...]
    for step in range(steps):
        for c in copies(step):
            c.wait()
        total = dot(lhs[...], held[step])
        at = step * block
        own_ref[:, at : at + block] = total[:keep]
        sent_ref[:, at : at + block] = total[keep:].astype(BF)


def in_hbm(pieces):
    return [pl.BlockSpec(memory_space=pltpu.HBM)] * len(pieces)


def rows_product(place, lhs, coded, pieces, block, with_squares):
    rows, depth = lhs.shape
    keep = rows // 2
    width = pieces[0].shape[1]
    sent = width + (128 if with_squares else 0)
    whole = lambda j, p: (0, 0)
    return pl.pallas_call(
        rows_kernel,
        grid_spec=pltpu.PrefetchScalarGridSpec(
            num_scalar_prefetch=1,
            grid=(1,),
            in_specs=[pl.BlockSpec(lhs.shape, whole), pl.BlockSpec(coded.shape, whole)] + in_hbm(pieces),
            out_specs=[pl.BlockSpec((keep, sent), whole), pl.BlockSpec((keep, width), whole)],
            scratch_shapes=[pltpu.VMEM((width // block, depth, block), BF), pltpu.SemaphoreType.DMA((width // block, OCT))],
        ),
        out_shape=[jax.ShapeDtypeStruct((keep, sent), BF), jax.ShapeDtypeStruct((keep, width), F32)],
        compiler_params=pltpu.CompilerParams(vmem_limit_bytes=VMEM),
    )(place, lhs, coded, *pieces)


def first_rows_kernel(place, lhs, coded_ref, *refs):
    weights, sent_refs, own_ref = refs[:12], refs[12:15], refs[15]
    step = pl.program_id(0)
    block = weights[0].shape[-1]
    keep, width = own_ref.shape

    @pl.when(step == 0)
    def _():
        for g, sent_ref in enumerate(sent_refs):
            sent_ref[:, width:] = coded_ref[g * keep : (g + 1) * keep]

    for i in range(3):
        total = None
        for k in range(4):
            term = dot(lhs[place[0] ^ k], weights[4 * i + k][...])
            total = term if total is None else total + term
        columns = pl.ds(pl.multiple_of(i * (width // 3) + step * block, 128), block)
        own_ref[:, columns] = total[:keep]
        for g, sent_ref in enumerate(sent_refs):
            sent_ref[:, columns] = total[(g + 1) * keep : (g + 2) * keep].astype(BF)


def first_rows_product(place, lhs, coded, pieces, block):
    _, rows, wide = lhs.shape
    keep = rows // 4
    each = pieces[0].shape[1]
    width = 3 * each
    whole = lambda j, p: (0, 0)
    sent = jax.ShapeDtypeStruct((keep, width + 128), BF)
    return pl.pallas_call(
        first_rows_kernel,
        grid_spec=pltpu.PrefetchScalarGridSpec(
            num_scalar_prefetch=1,
            grid=(each // block,),
            in_specs=[pl.BlockSpec(lhs.shape, lambda j, p: (0, 0, 0)), pl.BlockSpec(coded.shape, whole)]
            + [pl.BlockSpec((wide, block), lambda j, p: (0, j))] * len(pieces),
            out_specs=[pl.BlockSpec(sent.shape, whole)] * 3 + [pl.BlockSpec((keep, width), whole)],
        ),
        out_shape=[sent] * 3 + [jax.ShapeDtypeStruct((keep, width), F32)],
        compiler_params=pltpu.CompilerParams(vmem_limit_bytes=VMEM_ALL),
    )(place, lhs, coded, *pieces)


def columns_kernel(place, own_ref, got_ref, *refs):
    weights, (out_ref, parts, a_ref, held, sems) = refs[:OCT], refs[OCT:]
    keep, depth = own_ref.shape
    wide = held.shape[2] // 2
    copies = [pltpu.make_async_copy(w, held.at[n], sems.at[n]) for n, w in enumerate(weights)]
    for c in copies:
        c.start()
    a_ref[:keep] = own_ref[...]
    a_ref[keep:] = got_ref[...]
    below, above = wide // 128 * 128, -(-wide // 128) * 128
    for k in range(OCT):
        copies[k].wait()
        lower = dot(a_ref[:, : depth // 2], held[k, :, :above])
        upper = dot(a_ref[:, depth // 2 :], held[k, :, below:])
        parts[place[0] ^ k] = (lower[:, :wide] + upper[:, wide - below :]).astype(BF)
    for i in range(OCT):
        out_ref[:, i * wide : (i + 1) * wide] = parts[i]


def columns_product(place, own, got, pieces):
    keep, depth = own.shape
    rows = 2 * keep
    deep, double = pieces[0].shape
    wide = double // 2
    whole = lambda j, p: (0, 0)
    return pl.pallas_call(
        columns_kernel,
        grid_spec=pltpu.PrefetchScalarGridSpec(
            num_scalar_prefetch=1,
            grid=(1,),
            in_specs=[pl.BlockSpec((keep, depth), whole)] * 2 + in_hbm(pieces),
            out_specs=pl.BlockSpec((rows, OCT * wide), whole),
            scratch_shapes=[
                pltpu.VMEM((OCT, rows, wide), BF),
                pltpu.VMEM((rows, depth), BF),
                pltpu.VMEM((OCT, deep, double), BF),
                pltpu.SemaphoreType.DMA((OCT,)),
            ],
        ),
        out_shape=jax.ShapeDtypeStruct((rows, OCT * wide), BF),
        compiler_params=pltpu.CompilerParams(vmem_limit_bytes=VMEM),
    )(place, own, got, *pieces)


def out_kernel(place, own_ref, got_ref, *refs):
    weights, (out_ref, parts, a_ref) = refs[:OCT], refs[OCT:]
    keep, depth = own_ref.shape
    a_ref[:keep] = own_ref[...]
    a_ref[keep:] = got_ref[...]
    wide = weights[0].shape[-1] // 2
    below, above = wide // 128 * 128, -(-wide // 128) * 128
    for k in range(OCT):
        lower = dot(a_ref[:, : depth // 2], weights[k][:, :above])
        upper = dot(a_ref[:, depth // 2 :], weights[k][:, below:])
        parts[place[0] ^ k] = (lower[:, :wide] + upper[:, wide - below :]).astype(BF)
    for i in range(OCT):
        out_ref[:, i * wide : (i + 1) * wide] = parts[i]


def out_product(place, own, got, pieces):
    keep, depth = own.shape
    rows = 2 * keep
    deep, double = pieces[0].shape
    wide = double // 2
    whole = lambda j, p: (0, 0)
    return pl.pallas_call(
        out_kernel,
        grid_spec=pltpu.PrefetchScalarGridSpec(
            num_scalar_prefetch=1,
            grid=(1,),
            in_specs=[pl.BlockSpec((keep, depth), whole)] * 2 + [pl.BlockSpec((deep, double), whole)] * OCT,
            out_specs=pl.BlockSpec((rows, OCT * wide), whole),
            scratch_shapes=[pltpu.VMEM((OCT, rows, wide), BF), pltpu.VMEM((rows, depth), BF)],
        ),
        out_shape=jax.ShapeDtypeStruct((rows, OCT * wide), BF),
        compiler_params=pltpu.CompilerParams(vmem_limit_bytes=VMEM_ALL),
    )(place, own, got, *pieces)


def attention_kernel(model, *refs):
    own, *got = refs[:4]
    squares, cosine, left, right, seg_row, seg_col, slot, out_ref, keys_ref, values_ref = refs[4:]
    count, width = out_ref.shape
    heads_here = width // HEAD_DIM
    total = squares[:, :1]
    for g in got:
        last = g[:, 3 * width :].astype(F32)
        total = total + last[:, :1] + last[:, 64:65]
    scale = lax.rsqrt(total / model + EPS)

    def part(i):
        columns = slice(i * width, (i + 1) * width)
        x = own[:, columns]
        for g in got:
            x = x + g[:, columns].astype(F32)
        return x * scale

    query, key, value = part(0), part(1), part(2)

    def rotated(x):
        ahead = pltpu.roll(x, width - HEAD_DIM // 2, 1)
        behind = pltpu.roll(x, HEAD_DIM // 2, 1)
        return (x * cosine[...] + ahead * left[...] + behind * right[...]).astype(BF)

    q_rot, k_rot, v_b = rotated(query), rotated(key), value.astype(BF)
    spot = lax.broadcasted_iota(jnp.int32, (count, count), 0)
    hot = jnp.where(spot == slot[...], 1.0, 0.0).astype(BF)
    keys_ref[...] = dot(hot, k_rot).astype(BF)
    values_ref[...] = dot(hot, v_b).astype(BF)
    lane = lax.broadcasted_iota(jnp.int32, (count, width), 1)
    within = [(lane >= h * HEAD_DIM) & (lane < (h + 1) * HEAD_DIM) for h in range(heads_here)]
    zero = jnp.zeros((count, width), BF)
    spread_q = jnp.concatenate([jnp.where(w, q_rot, zero) for w in within], axis=0)
    scores = lax.dot_general(spread_q, k_rot, (((1,), (1,)), ((), ())), preferred_element_type=F32)
    scores = (scores * (1.0 / HEAD_DIM**0.5)).reshape(heads_here, count, count)
    other = lax.broadcasted_iota(jnp.int32, (count, count), 1)
    allowed = (seg_col[...] == seg_row[...]) & (other <= spot)
    scores = jnp.where(allowed[None], scores, -1e30)
    expo = jnp.exp(scores - jnp.max(scores, axis=-1, keepdims=True))
    probs = (expo / jnp.sum(expo, axis=-1, keepdims=True)).astype(BF)
    mixed = dot(probs.reshape(heads_here * count, count), v_b)
    total = jnp.zeros((count, width), F32)
    for h in range(heads_here):
        total = total + jnp.where(within[h], mixed[h * count : (h + 1) * count], 0.0)
    out_ref[...] = total.astype(BF)


def attend(model, own, got, squares, tables, segment, slots):
    count, width = own.shape[0], own.shape[1] // 3
    out = jax.ShapeDtypeStruct((count, width), BF)
    return pl.pallas_call(
        functools.partial(attention_kernel, model),
        out_shape=[out, out, out],
        compiler_params=pltpu.CompilerParams(vmem_limit_bytes=VMEM_ALL),
    )(own, *got, squares, *tables, segment.reshape(1, count), segment.reshape(count, 1), slots.reshape(1, count))


def rotation_tables(segment, width):
    half = HEAD_DIM // 2
    lane = jnp.arange(width, dtype=jnp.int32)
    freq = 10000.0 ** (-2.0 * (lane % half).astype(F32) / HEAD_DIM)
    angle = positions(segment).astype(F32)[:, None] * freq[None, :]
    first = ((lane % HEAD_DIM) < half)[None, :]
    sine = jnp.sin(angle)
    return jnp.cos(angle), jnp.where(first, -sine, 0.0), jnp.where(first, 0.0, sine)


def after(x, *others):
    return lax.optimization_barrier((x,) + others)[0]


def octet_plan(n_group):
    def swap(bit):
        pairs = [(g, g ^ bit) for g in range(n_group)]
        return lambda x: lax.ppermute(x, "group", pairs)

    core, near, next_to, across = swap(1), swap(2), swap(4), swap(OCT)

    def other_head(x):
        return lax.ppermute(x, "head", [(0, 1), (1, 0)])

    def beside(w):
        depth = w.shape[0]
        return jnp.concatenate([w[: depth // 2], w[depth // 2 :]], axis=1)

    def all_pieces(own, x, z, diagonal, early=(), late=()):
        return [
            own, core(after(own, *early)), x, core(after(x, *early)), z, core(after(z, *early)),
            diagonal, core(after(diagonal, *late)),
        ]

    def turn(k):
        pairs = [(g, (g + k * QUAD) % n_group) for g in range(n_group)]
        return lambda x: lax.ppermute(x, "group", pairs)

    turns = [turn(k) for k in range(4)]

    def per_device(
        tokens, attn_gain, w_query, w_key, w_value, w_out, mlp_gain, w_gate, w_up, w_down, segment_ids, cache_slot,
    ):
        group = lax.axis_index("group")
        side, fourth = group // OCT, group // QUAD
        place = (group % OCT).astype(jnp.int32).reshape(1)
        place4 = (group % QUAD).astype(jnp.int32).reshape(1)
        row = lax.axis_index("head")
        at_row = row.astype(jnp.int32).reshape(1)
        mine, model = tokens.shape
        half, quarter = model // 2, model // 4
        units = w_gate.shape[1]
        width = w_query.shape[1]
        tables = rotation_tables(segment_ids[0], width)
        gain1 = lax.dynamic_slice(attn_gain, (fourth * quarter,), (quarter,)).reshape(1, quarter)
        gain2 = lax.dynamic_slice(mlp_gain, (side * half,), (half,)).reshape(1, half)

        def columns_of(place, wide):
            return lax.dynamic_slice(tokens, (0, place * wide), (mine, wide))

        cut = [columns_of((fourth + k) % 4, quarter) for k in range(4)]
        given = columns_of(1 - side, half)
        cut = lax.optimization_barrier((*cut, given))
        came = [turns[k](cut[k]) for k in (3, 2, 1)]
        x_q, x_k, x_v = near(w_query), near(w_key), near(w_value)
        o_own, d_own = lax.optimization_barrier((beside(w_out), beside(w_down)))
        x_o = near(o_own)
        both = jnp.stack([cut[0], *came])
        partner = across(after(cut[4], both))
        gate, up, z_own = lax.optimization_barrier((w_gate, w_up, o_own, both, partner))[:3]
        z_o, z_g, z_u = next_to(z_own), next_to(gate), next_to(up)
        mine_too = jnp.stack([columns_of(side, half), partner])
        others_too = other_head(mine_too)
        others = other_head(after(both, x_q, gain1, gain2, *tables, z_g, others_too))
        _, lhs, coded, squares = prepare(
            first_kernel, at_row, (both, others, gain1), 8 * mine, quarter, 2 * mine, QUAD, VMEM_ALL
        )
        x_gate, x_up, x_down = lax.optimization_barrier((w_gate, w_up, d_own, x_q, x_k, x_v, x_o, both))[:3]
        x_g, x_u, x_d = near(x_gate), near(x_up), near(x_down)
        pieces = [p for w, x in ((w_query, x_q), (w_key, x_k), (w_value, x_v)) for p in (w, core(w), x, core(x))]
        *sent, own = first_rows_product(place4, after(lhs, partner), coded, pieces, 384)
        *sent, _ = lax.optimization_barrier((*sent, z_o, z_u))[:4]
        got = [turns[k + 1](sent[k]) for k in range(3)]
        d_o = near(after(z_o, sent[0]))
        got = lax.optimization_barrier((*got, d_o, x_g, x_u, x_d))[:3]
        p_o = all_pieces(o_own, x_o, z_o, d_o, (sent[0],), (sent[0],))
        attended, cache_keys, cache_values = attend(model, own, got, squares, tables, segment_ids[0], cache_slot[0])
        d_g, d_u = near(after(z_g, attended)), near(after(z_u, attended))
        got = across(attended)
        z_d = next_to(after(d_own, got))
        terms = out_product(place, attended, got, p_o)
        others = other_head(terms)
        p_g = all_pieces(w_gate, x_g, z_g, d_g, (attended,), (others,))
        middle, lhs, coded, squares = prepare(
            middle_kernel, at_row, (mine_too, others_too, terms, after(others, z_d, d_g), gain2), 4 * mine, half, 2 * mine, 1
        )
        sent_g, own_g = rows_product(place, lhs, coded, p_g, 512, True)
        got_g = across(sent_g)
        p_u = all_pieces(w_up, x_u, z_u, d_u, (lhs,), (got_g,))
        sent_u, own_u = rows_product(place, after(lhs, sent_g), coded, p_u, 512, False)
        got_u = across(sent_u)
        d_d = near(after(z_d, sent_g))
        p_d = all_pieces(d_own, x_d, z_d, d_d, (sent_u,), (got_u,))
        last = got_g[:, units:].astype(F32)
        scale = lax.rsqrt((squares[:, :1] + last[:, :1] + last[:, 64:65]) / model + EPS)
        gate = (own_g + got_g[:, :units].astype(F32)) * scale
        up = (own_u + got_u.astype(F32)) * scale
        hidden = (jax.nn.silu(gate) * up).astype(BF)
        terms = columns_product(place, hidden, across(hidden), p_d).reshape(2, 2, mine, half)
        given = other_head(lax.dynamic_index_in_dim(terms, 1 - row, 1, keepdims=False))
        mlp = lax.dynamic_index_in_dim(terms, row, 1, keepdims=False).astype(F32) + given.astype(F32)
        kept = lax.dynamic_index_in_dim(middle.reshape(2, 2, mine, half), row, 1, keepdims=False)
        out = (kept.astype(F32) + mlp).astype(BF)
        got = across(out[1])
        layer_out = jnp.where(
            side == 0, jnp.concatenate([out[0], got], axis=1), jnp.concatenate([got, out[0]], axis=1)
        )
        return (layer_out, cache_keys, cache_values)

    return per_device


def solution(mesh):
    n_group = mesh.shape["group"]
    in_specs = (
        P(("group", "head"), None),
        P(),
        P("group", "head"),
        P("group", "head"),
        P("group", "head"),
        P("head", "group"),
        P(),
        P("group", "head"),
        P("group", "head"),
        P("head", "group"),
        P("group", None),
        P("group", None),
    )
    out_specs = (P(("group", "head"), None), P("group", "head"), P("group", "head"))
    body = octet_plan(n_group) if n_group == 2 * OCT else gathered_plan
    return jax.shard_map(body, mesh=mesh, in_specs=in_specs, out_specs=out_specs, check_vma=False)
```
